128 devices in a mesh: leaf: 4 (over z), dev: 32 (over y, x, core).
Axes of the slice: x: 4, y: 4, z: 4, core: 2. Of those that a mesh axis runs over, the one named last changes fastest.
Arguments:
- panel_coords: float32 [3, 2097152], P(None, ('leaf', 'dev')), may hold values from -2 to 2
- panel_weights: float32 [2097152], P(('leaf', 'dev')), may hold values from 0.25 to 4
- panel_order: int32 [128, 16384], P(('leaf', 'dev')), may hold values from 0 to 16383, each once within a row
- row_owner: int32 [4096, 1], P(('leaf', 'dev')), may hold values from 0 to 31; in each aligned block of 32 rows (0 to 31, 32 to 63, ...) at most 2 rows name the same one
- col_owner: int32 [4096, 1], P(('leaf', 'dev')), may hold values from 0 to 31; in each aligned block of 32 rows (0 to 31, 32 to 63, ...) at most 2 rows name the same one
- pair_slots: int32 [4096, 2], P(('leaf', 'dev')), may hold values from 0 to 15
- rank_blocks: int32 [4096], P(('leaf', 'dev')), may hold values from 1 to 4
- sketch: bfloat16 [4096, 1024, 128], P(('leaf', 'dev')), may hold values from -0.1875 to 0.1875
Outputs:
- range_sketch: bfloat16 [4096, 1024, 128], P(('leaf', 'dev'))
- co_sketch: bfloat16 [4096, 128, 1024], P(('leaf', 'dev'))
The draws below stay inside these ranges and needn't reach their ends.
Inputs may be any that keep to these rules, and one draw needn't show every extreme that they name: `row_owner`: in the rows of one device, each value is named by at most 2 rows; the value is a member index inside the device's own subtree group. `col_owner`: in the rows of one device, each value is named by at most 2 rows; the value is a member index inside the device's own subtree group. `panel_order`: each row is a permutation.
All inputs are finite; a program needn't handle non-finite values.
Results may differ from the reference program's by a relative error of at most 0.005.
Values sent between devices are 32-bit elements; how exact they have to be, the bound alone decides.
No kernel may reach another device: no remote copies, remote signals or barrier semaphores. Data moves between devices by JAX's collectives and lax.ppermute only.
A program may use at most 192 MiB of HBM per device.

```python
import math
import jax
import jax.numpy as jnp
import numpy as np
from jax import lax

PTS = 1024
RK = 128
BLK = 32
CL_DEV = 16
PAIRS_DEV = 32
CAP = 2
PAIRS = 4096
NPANELS = 2097152
N_LEAF = 4
N_DEV = 32


def touch_ends(result, key, smallest, largest):
    index_at = [jax.random.randint(jax.random.fold_in(key, axis), (), 0, length) for axis, length in enumerate(result.shape)]
    widest = result.shape.index(max(result.shape))
    beside = index_at[:widest] + [(index_at[widest] + 1) % result.shape[widest]] + index_at[widest + 1:]
    return result.at[tuple(index_at)].set(smallest).at[tuple(beside)].set(largest)


def levels(own_key, dims, shards, least, top_value):
    def one(axis_at, parts):
        heights = jax.random.uniform(jax.random.fold_in(jax.random.fold_in(own_key, 6), axis_at), (parts,), jnp.float32, least / len(shards), top_value / len(shards))
        return jnp.repeat(jnp.exp(heights), dims[axis_at] // parts).reshape((-1,) + (1,) * (len(dims) - axis_at - 1))

    factor_of = one(*shards[0])
    for cut in shards[1:]:
        factor_of = factor_of * one(*cut)
    return factor_of


def assign_block(key, own, number, rows, amount, top, most, lean):
    order = jax.random.permutation(key, amount)
    heavy_load, ordinary = portions_of(amount, rows * top, most, lean, True), portions_of(amount, rows * top, most, lean, False)
    places = jnp.arange(amount)

    def named(lengths, offset_by):
        used = int((lengths > 0).sum())
        fixed = max(1, used // 4)
        passed = fixed + (places - fixed + offset_by * (used - fixed)) % max(1, amount - fixed)
        return jnp.zeros((amount,), jnp.int32).at[order[jnp.where(places < fixed, places, passed)]].set(jnp.asarray(lengths, jnp.int32))

    lengths = jnp.where(number % 4 == 0, named(heavy_load, number // 4), named(ordinary, number - number // 4 - 1))
    mixed = jax.random.permutation(jax.random.fold_in(own, 3), amount)
    giver, sink = mixed[0:amount // 2 * 2:2], mixed[1:amount // 2 * 2:2]
    room = jnp.minimum(lengths[giver] - 1, most - lengths[sink]) // 2
    room = jnp.where((giver == order[0]) | (sink == order[0]) | (lengths[sink] == 0), 0, jnp.maximum(room, 0))
    passed = jax.random.randint(jax.random.fold_in(own, 4), (amount // 2,), 0, 1 << 20) % (room + 1)
    lengths = lengths.at[giver].add(-passed).at[sink].add(passed)
    items = jnp.searchsorted(jnp.cumsum(lengths), jnp.arange(rows * top), side="right").astype(jnp.int32)
    grid = items.reshape(top, rows).T
    grid = grid[jax.random.permutation(jax.random.fold_in(own, 1), rows)]
    offset_by = jax.random.randint(jax.random.fold_in(own, 2), (rows, 1), 0, top)
    return jnp.take_along_axis(grid, (jnp.arange(top)[None, :] + offset_by) % top, axis=1)


def portions_of(number_of, total, limit, slope, full):
    weights = [(1 << 20) // math.isqrt(rank ** slope) + 1 for rank in range(1, number_of + 1)]
    largest = limit if full else min(limit, max(-(-total // number_of), total * weights[0] // sum(weights)))
    least = 1 if total - largest >= number_of - 1 else 0
    counts, rest = [largest] + [least] * (number_of - 1), total - largest - least * (number_of - 1)
    while rest > 0:
        free = [i for i in range(1, number_of) if counts[i] < largest] or [i for i in range(1, number_of) if counts[i] < limit]
        mass, budget = sum([weights[i] for i in free]), rest
        for i in free:
            extra = min(limit - counts[i], max(1, budget * weights[i] // mass), rest)
            counts[i] = counts[i] + extra
            rest = rest - extra
    return np.array(counts)


def gaussian(own_key, extent, scale, most, split=(), kind=jnp.bfloat16):
    array = scale * jax.random.normal(own_key, extent, jnp.float32)
    if split:
        array = array * levels(own_key, extent, split, -0.22, 0.18)
    return jnp.clip(array, -most, most).astype(kind)


def setup_inputs(seed: int = 0) -> dict:
    seeds = jax.random.split(jax.random.key(seed), 9)
    panel_coords = jnp.clip(jax.random.uniform(seeds[0], (3, NPANELS), jnp.float32, -2.0, 2.0) * levels(seeds[0], (3, NPANELS), ((1, 128),), -0.4, 0.0), -2.0, 2.0)
    panel_weights = jnp.clip(jnp.exp(math.log(4.0) - 2.7725887 * jax.random.uniform(seeds[1], (NPANELS,), jnp.float32) ** levels(seeds[1], (NPANELS,), ((0, 128),), -0.2, 0.2)), 0.25, 4.0)
    panel_order = jax.vmap(lambda own: jax.random.permutation(own, CL_DEV * PTS))(jax.random.split(seeds[2], (N_LEAF * N_DEV))).reshape((N_LEAF * N_DEV, CL_DEV * PTS)).astype(jnp.int32)
    row_owner_keys = jax.random.split(jax.random.fold_in(seeds[3], 1), PAIRS // PAIRS_DEV)
    row_owner_turns = jax.random.permutation(jax.random.fold_in(seeds[3], 3), PAIRS // PAIRS_DEV)
    row_owner = jax.vmap(lambda own, number: assign_block(jax.random.fold_in(seeds[3], 2), own, number, PAIRS_DEV, N_DEV, 1, CAP, 2))(row_owner_keys, row_owner_turns).reshape((PAIRS, 1))
    col_owner_keys = jax.random.split(jax.random.fold_in(seeds[4], 1), PAIRS // PAIRS_DEV)
    col_owner_turns = jax.random.permutation(jax.random.fold_in(seeds[4], 3), PAIRS // PAIRS_DEV)
    col_owner = jax.vmap(lambda own, number: assign_block(jax.random.fold_in(seeds[4], 2), own, number, PAIRS_DEV, N_DEV, 1, CAP, 1))(col_owner_keys, col_owner_turns).reshape((PAIRS, 1))
    pair_slots = touch_ends(jax.random.randint(seeds[5], (PAIRS, 2), 0, CL_DEV), jax.random.fold_in(seeds[5], 1), 0, CL_DEV - 1).astype(jnp.int32)
    rank_blocks = touch_ends(jax.random.randint(seeds[6], (PAIRS,), 1, RK // BLK + 1), jax.random.fold_in(seeds[6], 1), 1, (RK // BLK + 1) - 1).astype(jnp.int32)
    sketch = gaussian(seeds[7], (PAIRS, PTS, RK), PTS ** -0.5, 0.1875, ((0, 128),))
    return dict(panel_coords=panel_coords, panel_weights=panel_weights, panel_order=panel_order, row_owner=row_owner, col_owner=col_owner, pair_slots=pair_slots, rank_blocks=rank_blocks, sketch=sketch)


softening = 0.01

def interaction(row_points, col_points):
    delta_x = row_points[0][:, None] - col_points[0][None, :]
    delta_y = row_points[1][:, None] - col_points[1][None, :]
    delta_z = row_points[2][:, None] - col_points[2][None, :]
    squared = delta_x * delta_x + delta_y * delta_y + delta_z * delta_z + softening
    return (col_points[3][None, :] / jnp.sqrt(squared)).astype(jnp.bfloat16)

def pair_sketch(row_points, col_points, test_matrix, rank):
    kernel = interaction(row_points, col_points)
    active = lax.broadcasted_iota(jnp.int32, (1, test_matrix.shape[1]), 1) < rank * BLK
    masked = jnp.where(active, test_matrix, jnp.zeros_like(test_matrix))
    ranged = jnp.dot(kernel, masked, preferred_element_type=jnp.float32).astype(jnp.bfloat16)
    scale = 1.0 / math.sqrt(kernel.shape[0])
    product = lax.dot_general(ranged, kernel, (((0,), (0,)), ((), ())), preferred_element_type=jnp.float32)
    return (ranged, (product * scale).astype(jnp.bfloat16))

def cluster_points(panel_coords, panel_weights, panel_order):
    devices = panel_order.shape[0]
    span = panel_order.shape[1]
    offsets = (jnp.arange(devices, dtype=jnp.int32) * span)[:, None]
    index = (panel_order + offsets).reshape(-1)
    coords = jnp.take(panel_coords, index, axis=1)
    weights = jnp.take(panel_weights, index)
    stacked = jnp.concatenate([coords, weights[None, :]], axis=0)
    return stacked.reshape(4, -1, PTS).transpose(1, 0, 2)

def reference(panel_coords, panel_weights, panel_order, row_owner, col_owner, pair_slots, rank_blocks, sketch):
    points = cluster_points(panel_coords, panel_weights, panel_order)
    count = rank_blocks.shape[0]
    device_of = jnp.arange(count, dtype=jnp.int32) // PAIRS_DEV
    base = device_of // N_DEV * (N_DEV * CL_DEV)
    row_id = (base + row_owner[:, 0] * CL_DEV + pair_slots[:, 0]).astype(jnp.int32)
    col_id = (base + col_owner[:, 0] * CL_DEV + pair_slots[:, 1]).astype(jnp.int32)

    def single(operands):
        row_index, col_index, test_matrix, rank = operands
        return pair_sketch(points[row_index], points[col_index], test_matrix, rank)
    range_sketch, co_sketch = lax.map(single, (row_id, col_id, sketch, rank_blocks))
    return (range_sketch, co_sketch)
```

```python
import functools
import math

import jax
import jax.numpy as jnp
from jax import lax
from jax.experimental import pallas as pl
from jax.experimental.pallas import tpu as pltpu
from jax.sharding import PartitionSpec as P

PTS = 1024
RK = 128
BLK = 32
CL_DEV = 16
CHUNK = 256

softening = 0.01
bf16 = jnp.bfloat16
f32 = jnp.float32


def contract(a, b, dim_a, dim_b):
    return lax.dot_general(a, b, (((dim_a,), (dim_b,)), ((), ())), preferred_element_type=f32)


def pick_kernel(order_ref, coords_ref, weights_ref, out_ref):
    unroll = 32
    for cluster in range(CL_DEV):
        index = order_ref[cluster * 8 : cluster * 8 + 8, :]
        high = index >> 7
        low = index & 127

        def step(turn, picked):
            picked = list(picked)
            for inner in range(unroll):
                row = turn * unroll + inner
                here = high == row
                for part in range(4):
                    if part < 3:
                        line = coords_ref[part, pl.ds(row, 1), :]
                    else:
                        line = weights_ref[pl.ds(row, 1), :]
                    line = jnp.broadcast_to(line, (8, 128))
                    found = jnp.take_along_axis(line, low, axis=1, mode="promise_in_bounds")
                    picked[part] = jnp.where(here, found, picked[part])
            return tuple(picked)

        zero = jnp.zeros((8, 128), f32)
        picked = lax.fori_loop(0, 128 // unroll, step, (zero,) * 4)
        for part in range(4):
            for line in range(8):
                out_ref[cluster, part : part + 1, line * 128 : line * 128 + 128] = picked[part][
                    line : line + 1, :
                ]


def pick(order, coords, weights):
    return pl.pallas_call(
        pick_kernel,
        out_shape=jax.ShapeDtypeStruct((CL_DEV, 4, PTS), f32),
        in_specs=[pl.BlockSpec(memory_space=pltpu.VMEM)] * 3,
        out_specs=pl.BlockSpec(memory_space=pltpu.VMEM),
        name="pick",
    )(order, coords, weights)


def reply_kernel(wanted_ref, points_ref, out_ref):
    first = pl.program_id(0) * out_ref.shape[0]
    for slot in range(out_ref.shape[0]):
        out_ref[slot] = points_ref[wanted_ref[first + slot]]


def reply(wanted, points):
    slots = wanted.shape[0]
    step = 16
    return pl.pallas_call(
        reply_kernel,
        grid_spec=pltpu.PrefetchScalarGridSpec(
            num_scalar_prefetch=1,
            grid=(slots // step,),
            in_specs=[pl.BlockSpec((CL_DEV, 4, PTS), lambda i, wanted: (0, 0, 0))],
            out_specs=pl.BlockSpec((step, 4, PTS), lambda i, wanted: (i, 0, 0)),
        ),
        out_shape=jax.ShapeDtypeStruct((slots, 4, PTS), f32),
        name="reply",
    )(wanted, points)


def split3(value):
    first = value.astype(bf16).astype(f32)
    rest = value - first
    second = rest.astype(bf16).astype(f32)
    return first, second, rest - second


def distance_operands(rows, cols):
    line = lax.broadcasted_iota(jnp.int32, (4, PTS), 0)
    row_square = rows[0:1] * rows[0:1] + rows[1:2] * rows[1:2] + rows[2:3] * rows[2:3]
    left = jnp.where(line < 3, rows, row_square)
    inverse = 1.0 / (cols[3:4] * cols[3:4])
    col_square = cols[0:1] * cols[0:1] + cols[1:2] * cols[1:2] + cols[2:3] * cols[2:3]
    right = jnp.where(line < 3, cols * (-2.0 * inverse), inverse)
    l1, l2, l3 = split3(left)
    r1, r2, r3 = split3(right)
    c1, c2, c3 = split3((col_square + softening) * inverse)
    ones = jnp.ones((4, PTS), f32)
    zero = jnp.zeros((4, PTS), f32)
    last = jnp.where(line == 0, c1, jnp.where(line == 1, c2, jnp.where(line == 2, c3, 0.0)))
    left = jnp.concatenate([l1, l1, l2, l1, l2, l3, ones, zero], axis=0).astype(bf16)
    right = jnp.concatenate([r1, r2, r1, r3, r2, r1, last, zero], axis=0).astype(bf16)
    return left, right


def pair_kernel(row_at, col_at, rank, rows_ref, cols_ref, sketch_ref, range_ref, co_ref):
    left, right = distance_operands(rows_ref[0], cols_ref[0])
    limit = rank[pl.program_id(0)] * BLK
    test = sketch_ref[0]
    active = lax.broadcasted_iota(jnp.int32, (1, RK), 1) < limit
    masked = jnp.where(active, test, jnp.zeros_like(test)).T

    def block(chunk):
        part = left[:, chunk * CHUNK : (chunk + 1) * CHUNK]
        return lax.rsqrt(contract(right, part, 0, 0)).astype(bf16)

    total = None
    now = block(0)
    for chunk in range(PTS // CHUNK):
        later = block(chunk + 1) if chunk + 1 < PTS // CHUNK else None
        ranged = contract(masked, now, 1, 0).astype(bf16)
        range_ref[0, chunk * CHUNK : (chunk + 1) * CHUNK, :] = ranged.T
        product = contract(ranged, now, 1, 1)
        total = product if total is None else total + product
        now = later
    co_ref[0] = (total * (1.0 / math.sqrt(PTS))).astype(bf16)


def pair_products(row_at, col_at, rank, replies, sketch):
    count = sketch.shape[0]
    return pl.pallas_call(
        pair_kernel,
        grid_spec=pltpu.PrefetchScalarGridSpec(
            num_scalar_prefetch=3,
            grid=(count,),
            in_specs=[
                pl.BlockSpec((1, 4, PTS), lambda p, row, col, rank: (row[p], 0, 0)),
                pl.BlockSpec((1, 4, PTS), lambda p, row, col, rank: (col[p], 0, 0)),
                pl.BlockSpec((1, PTS, RK), lambda p, row, col, rank: (p, 0, 0)),
            ],
            out_specs=[
                pl.BlockSpec((1, PTS, RK), lambda p, row, col, rank: (p, 0, 0)),
                pl.BlockSpec((1, RK, PTS), lambda p, row, col, rank: (p, 0, 0)),
            ],
        ),
        out_shape=[
            jax.ShapeDtypeStruct((count, PTS, RK), bf16),
            jax.ShapeDtypeStruct((count, RK, PTS), bf16),
        ],
        compiler_params=pltpu.CompilerParams(vmem_limit_bytes=48 << 20),
        name="pairs",
    )(row_at, col_at, rank, replies, replies, sketch)


def shards(
    panel_coords, panel_weights, panel_order, row_owner, col_owner, pair_slots, rank_blocks, sketch
):
    members = lax.axis_size("dev")
    me = lax.axis_index("dev")
    count = rank_blocks.shape[0]
    named = jnp.concatenate([row_owner, col_owner, pair_slots], axis=1).T
    everyone = lax.all_gather(named, "dev", axis=0, tiled=False)
    points = pick(
        panel_order.reshape(128, 128),
        panel_coords.reshape(3, 128, 128),
        panel_weights.reshape(128, 128),
    )
    mine = (everyone[:, :2, :] == me).astype(jnp.int32)
    before = jnp.cumsum(mine, axis=2) - mine
    nth = jnp.arange(2, dtype=jnp.int32)[None, None, :, None]
    chosen = mine[:, :, None, :] * (before[:, :, None, :] == nth)
    wanted = jnp.sum(chosen * everyone[:, 2:, None, :], axis=3)
    found = reply(wanted.reshape(-1), points).reshape(members, 4, 4, PTS)
    replies = lax.all_to_all(found, "dev", split_axis=0, concat_axis=0, tiled=True)
    owners = named[:2]
    same = owners[:, :, None] == owners[:, None, :]
    earlier = jnp.tril(jnp.ones((count, count), jnp.bool_), -1)
    position = jnp.sum((same & earlier[None]).astype(jnp.int32), axis=2)
    at = owners * 4 + jnp.arange(2, dtype=jnp.int32)[:, None] * 2 + position
    return tuple(
        pair_products(at[0], at[1], rank_blocks, replies.reshape(members * 4, 4, PTS), sketch)
    )


def solution(mesh):
    in_specs = (
        P(None, ("leaf", "dev")),
        P(("leaf", "dev")),
        P(("leaf", "dev"), None),
        P(("leaf", "dev"), None),
        P(("leaf", "dev"), None),
        P(("leaf", "dev"), None),
        P(("leaf", "dev")),
        P(("leaf", "dev"), None, None),
    )
    out_specs = (P(("leaf", "dev"), None, None), P(("leaf", "dev"), None, None))
    return jax.shard_map(shards, mesh=mesh, in_specs=in_specs, out_specs=out_specs, check_vma=False)
```

```python
import functools
import math

import jax
import jax.numpy as jnp
from jax import lax
from jax.experimental import pallas as pl
from jax.experimental.pallas import tpu as pltpu
from jax.sharding import PartitionSpec as P

PTS = 1024
RK = 128
BLK = 32
CL_DEV = 16

softening = 0.01
bf16 = jnp.bfloat16
f32 = jnp.float32


def contract(a, b, dim_a, dim_b):
    return lax.dot_general(a, b, (((dim_a,), (dim_b,)), ((), ())), preferred_element_type=f32)

LEVELS = 65535
PICK_UNROLL = 32


def pick_kernel(order_ref, coords_ref, weights_ref, out_ref, pack_ref):
    step = LEVELS / 4.0

    def fixed(value, low):
        return (value * step + (0.5 - low * step)).astype(jnp.int32)

    pack_ref[0] = (fixed(coords_ref[0], -2.0) << 16) | fixed(coords_ref[1], -2.0)
    pack_ref[1] = (fixed(coords_ref[2], -2.0) << 16) | fixed(weights_ref[...], 0.0)
    for cluster in range(CL_DEV):
        index = order_ref[cluster * 8 : cluster * 8 + 8, :]
        high = index >> 7
        low = index & 127

        def turn(number, picked):
            picked = list(picked)
            for inner in range(PICK_UNROLL):
                row = number * PICK_UNROLL + inner
                here = high == row
                for part in range(2):
                    line = jnp.broadcast_to(pack_ref[part, pl.ds(row, 1), :], (8, 128))
                    found = jnp.take_along_axis(line, low, axis=1, mode="promise_in_bounds")
                    picked[part] = jnp.where(here, found, picked[part])
            return tuple(picked)

        zero = jnp.zeros((8, 128), jnp.int32)
        picked = lax.fori_loop(0, 128 // PICK_UNROLL, turn, (zero, zero))
        values = []
        for part in range(2):
            values.append(((picked[part] >> 16) & LEVELS).astype(f32) * (1.0 / step) - 2.0)
            second = (picked[part] & LEVELS).astype(f32) * (1.0 / step)
            values.append(second - 2.0 if part == 0 else second)
        for part in range(4):
            for line in range(8):
                out_ref[cluster, part : part + 1, line * 128 : line * 128 + 128] = values[part][
                    line : line + 1, :
                ]


def pick(order, coords, weights):
    return pl.pallas_call(
        pick_kernel,
        out_shape=jax.ShapeDtypeStruct((CL_DEV, 4, PTS), f32),
        in_specs=[pl.BlockSpec(memory_space=pltpu.VMEM)] * 3,
        out_specs=pl.BlockSpec(memory_space=pltpu.VMEM),
        scratch_shapes=[pltpu.VMEM((2, 128, 128), jnp.int32)],
        cost_estimate=pl.CostEstimate(flops=40_000_000, bytes_accessed=600_000, transcendentals=0),
        name="pick",
    )(order, coords, weights)


def plan_kernel(named_ref, wanted_ref, places_ref):
    count = named_ref.shape[1]
    square = (count, count)
    named = named_ref[...].astype(f32)
    down = lax.broadcasted_iota(jnp.int32, square, 0)
    along = lax.broadcasted_iota(jnp.int32, square, 1)
    eye = down == along
    number = along.astype(f32)
    number_down = down.astype(f32)

    def column(row):
        return jnp.sum(jnp.where(eye, row, 0.0), axis=1, keepdims=True)

    def product(a, b):
        return jnp.where(contract(a, b, 1, 0) > 0.5, 1.0, 0.0).astype(bf16)

    row_owner, col_owner, row_slot, col_slot, rank = (named[i : i + 1] for i in range(5))
    same_row = jnp.where((column(row_owner) == row_owner) & ~eye, 1.0, 0.0)
    same_col = jnp.where((column(col_owner) == col_owner) & ~eye, 1.0, 0.0)
    either = (same_row + same_col).astype(bf16)
    same_row, same_col = same_row.astype(bf16), same_col.astype(bf16)
    steps = contract(same_row, same_col, 1, 0) + contract(same_col, same_row, 1, 0)
    alike = jnp.where(eye | (steps > 0.5), 1.0, 0.0).astype(bf16)
    for _ in range(4):
        alike = product(alike, alike)
    other = product(alike, either)
    far = float(2 * count)
    least = jnp.min(jnp.where(alike.astype(f32) > 0.5, number, far), axis=1, keepdims=True)
    least_other = jnp.min(jnp.where(other.astype(f32) > 0.5, number, far), axis=1, keepdims=True)
    first = jnp.where(least < least_other, 1.0, 0.0)
    size = jnp.sum(first, axis=0, keepdims=True)
    flip = size < count / 2
    first = jnp.where(flip, 1.0 - first, first)
    size = jnp.where(flip, count - size, size)
    first_row = jnp.sum(jnp.where(eye, first, 0.0), axis=0, keepdims=True)
    before = jnp.sum(jnp.where(along < down, first_row, 0.0), axis=1, keepdims=True)
    before_other = jnp.sum(jnp.where(along < down, 1.0 - first_row, 0.0), axis=1, keepdims=True)
    position = jnp.where(first > 0.5, before, size + before_other)
    hit = position == number

    def ordered(values):
        return jnp.sum(jnp.where(hit, values, 0.0), axis=0, keepdims=True)

    places = [
        ordered(number_down),
        ordered(column(row_owner * 2.0)),
        ordered(column(col_owner * 2.0 + 1.0)),
        ordered(column(rank)),
        ordered(1.0 - first),
    ]
    for line, value in enumerate(places):
        places_ref[line : line + 1, :] = value.astype(jnp.int32)
    places_ref[5:8, :] = jnp.zeros((3, count), jnp.int32)
    lane = lax.broadcasted_iota(jnp.int32, wanted_ref.shape, 1)
    wanted = jnp.zeros(wanted_ref.shape, f32)
    for phase in range(2):
        turn = first_row > 0.5 if phase == 0 else first_row < 0.5
        for side, (owner, slot) in enumerate(((row_owner, row_slot), (col_owner, col_slot))):
            value = jnp.sum(
                jnp.where((owner == number_down) & turn, slot, 0.0), axis=1, keepdims=True
            )
            wanted = jnp.where(lane == phase * 2 + side, value, wanted)
    wanted_ref[...] = wanted.astype(jnp.int32)


def plan(named, members):
    count = named.shape[1]
    return pl.pallas_call(
        plan_kernel,
        out_shape=[
            jax.ShapeDtypeStruct((members, 128), jnp.int32),
            jax.ShapeDtypeStruct((8, count), jnp.int32),
        ],
        in_specs=[pl.BlockSpec(memory_space=pltpu.VMEM)],
        out_specs=[pl.BlockSpec(memory_space=pltpu.VMEM)] * 2,
        name="plan",
    )(named)


def reply_kernel(phase, wanted_ref, points_ref, out_ref, sem):
    for member in range(out_ref.shape[0]):
        for side in range(2):
            pltpu.make_async_copy(
                points_ref.at[wanted_ref[member, phase * 2 + side]],
                out_ref.at[member, side],
                sem,
            ).start()
    pltpu.make_async_copy(out_ref, out_ref, sem).wait()


def reply(phase, wanted, points):
    members = wanted.shape[0]
    return pl.pallas_call(
        functools.partial(reply_kernel, phase),
        in_specs=[
            pl.BlockSpec(memory_space=pltpu.SMEM),
            pl.BlockSpec(memory_space=pltpu.VMEM),
        ],
        out_specs=pl.BlockSpec(memory_space=pltpu.HBM),
        out_shape=jax.ShapeDtypeStruct((members, 2, 4, PTS), f32),
        scratch_shapes=[pltpu.SemaphoreType.DMA],
        cost_estimate=pl.CostEstimate(flops=0, bytes_accessed=4_000_000, transcendentals=0),
        name="reply",
    )(wanted, points)


def split3(value):
    first = value.astype(bf16).astype(f32)
    rest = value - first
    second = rest.astype(bf16).astype(f32)
    return first, second, rest - second


def distance_operands(rows, cols):
    line = lax.broadcasted_iota(jnp.int32, (4, PTS), 0)
    row_square = rows[0:1] * rows[0:1] + rows[1:2] * rows[1:2] + rows[2:3] * rows[2:3]
    left = jnp.where(line < 3, rows, row_square)
    inverse = 1.0 / (cols[3:4] * cols[3:4])
    col_square = cols[0:1] * cols[0:1] + cols[1:2] * cols[1:2] + cols[2:3] * cols[2:3]
    right = jnp.where(line < 3, cols * (-2.0 * inverse), inverse)
    l1, l2, l3 = split3(left)
    r1, r2, r3 = split3(right)
    c1, c2, c3 = split3((col_square + softening) * inverse)
    ones = jnp.ones((4, PTS), f32)
    zero = jnp.zeros((4, PTS), f32)
    last = jnp.where(line == 0, c1, jnp.where(line == 1, c2, jnp.where(line == 2, c3, 0.0)))
    left = jnp.concatenate([l1, l1, l2, l1, l2, l3, ones, zero], axis=0).astype(bf16)
    right = jnp.concatenate([r1, r2, r1, r3, r2, r1, last, zero], axis=0).astype(bf16)
    return left, right


def pair_block(first, places, rows, cols, sketch_ref, range_ref, co_ref):
    left, right = distance_operands(rows, cols)
    limit = places[3, first + pl.program_id(0)] * BLK
    test = sketch_ref[0]
    active = lax.broadcasted_iota(jnp.int32, (1, RK), 1) < limit
    masked = jnp.where(active, test, jnp.zeros_like(test)).T
    block = lax.rsqrt(contract(right, left, 0, 0)).astype(bf16)
    ranged = contract(masked, block, 1, 0).astype(bf16)
    range_ref[0] = ranged.T
    co_ref[0] = (contract(ranged, block, 1, 1) * (1.0 / math.sqrt(PTS))).astype(bf16)


def early_kernel(places, rows_ref, cols_ref, sketch_ref, range_ref, co_ref):
    pair_block(0, places, rows_ref[0], cols_ref[0], sketch_ref, range_ref, co_ref)


def late_kernel(
    first, places, rows_0, cols_0, rows_1, cols_1, sketch_ref, old_range, old_co, range_ref, co_ref
):
    early = places[4, first + pl.program_id(0)] == 0
    rows = jnp.where(early, rows_0[0], rows_1[0])
    cols = jnp.where(early, cols_0[0], cols_1[0])
    pair_block(first, places, rows, cols, sketch_ref, range_ref, co_ref)


def pair_products(first, number, places, replies, sketch, old):
    count = sketch.shape[0]
    points = []
    for phase in range(len(replies)):
        for line in (1, 2):

            def at(p, places, phase=phase, line=line):
                place = places[line, first + p]
                if len(replies) > 1:
                    late = places[4, first + p]
                    place = place * (late if phase else 1 - late)
                return (place, 0, 0)

            points.append(pl.BlockSpec((1, 4, PTS), at))

    def own(p, places):
        return (places[0, first + p], 0, 0)

    pair_specs = [pl.BlockSpec((1, PTS, RK), own), pl.BlockSpec((1, RK, PTS), own)]
    operands = [places] + [reply for reply in replies for _ in range(2)] + [sketch] + list(old)
    body = functools.partial(late_kernel, first) if old else early_kernel
    return pl.pallas_call(
        body,
        grid_spec=pltpu.PrefetchScalarGridSpec(
            num_scalar_prefetch=1,
            grid=(number,),
            in_specs=points
            + pair_specs[:1]
            + [pl.BlockSpec(memory_space=pl.ANY) for _ in old],
            out_specs=pair_specs,
        ),
        out_shape=[
            jax.ShapeDtypeStruct((count, PTS, RK), bf16),
            jax.ShapeDtypeStruct((count, RK, PTS), bf16),
        ],
        input_output_aliases={len(operands) - 2: 0, len(operands) - 1: 1} if old else {},
        compiler_params=pltpu.CompilerParams(vmem_limit_bytes=48 << 20),
        cost_estimate=pl.CostEstimate(
            flops=number * 6 * PTS * PTS * 256, bytes_accessed=number * 800_000, transcendentals=0
        ),
        name="pairs",
    )(*operands)


def shards(
    panel_coords, panel_weights, panel_order, row_owner, col_owner, pair_slots, rank_blocks, sketch
):
    members = lax.axis_size("dev")
    count = rank_blocks.shape[0]
    named = jnp.concatenate(
        [row_owner, col_owner, pair_slots, rank_blocks[:, None], jnp.zeros((count, 3), jnp.int32)],
        axis=1,
    ).T
    wanted, places = plan(named, members)
    asked = lax.all_to_all(wanted, "dev", split_axis=0, concat_axis=0, tiled=True)
    points = pick(
        panel_order.reshape(128, 128),
        panel_coords.reshape(3, 128, 128),
        panel_weights.reshape(128, 128),
    )
    replies = []
    for phase in range(2):
        found = reply(phase, asked, points)
        got = lax.all_to_all(found, "dev", split_axis=0, concat_axis=0, tiled=True)
        replies.append(got.reshape(members * 2, 4, PTS))
    half = count // 2
    early = pair_products(0, half, places, replies[:1], sketch, ())
    return tuple(pair_products(half, count - half, places, replies, sketch, early))


def solution(mesh):
    in_specs = (
        P(None, ("leaf", "dev")),
        P(("leaf", "dev")),
        P(("leaf", "dev"), None),
        P(("leaf", "dev"), None),
        P(("leaf", "dev"), None),
        P(("leaf", "dev"), None),
        P(("leaf", "dev")),
        P(("leaf", "dev"), None, None),
    )
    out_specs = (P(("leaf", "dev"), None, None), P(("leaf", "dev"), None, None))
    return jax.shard_map(shards, mesh=mesh, in_specs=in_specs, out_specs=out_specs, check_vma=False)
```

```python
import functools
import math

import jax
import jax.numpy as jnp
from jax import lax
from jax.experimental import pallas as pl
from jax.experimental.pallas import tpu as pltpu
from jax.sharding import PartitionSpec as P

PTS = 1024
RK = 128
BLK = 32
CL_DEV = 16

softening = 0.01
bf16 = jnp.bfloat16
f32 = jnp.float32


def contract(a, b, dim_a, dim_b):
    return lax.dot_general(a, b, (((dim_a,), (dim_b,)), ((), ())), preferred_element_type=f32)

PICK_TURN = 2
LANES = 256


def pick_kernel(order_ref, coords_ref, weights_ref, out_ref, table_ref, split_ref):
    for part in range(3):
        for m in range(64):
            table_ref[part * 64 + m : part * 64 + m + 1, :] = coords_ref[
                part : part + 1, m * 256 : m * 256 + 256
            ]
    for half in range(2):
        table_ref[192:256, half * 128 : half * 128 + 128] = weights_ref[
            pl.ds(half, 64, stride=2), :
        ]
    table = table_ref[...]
    head = table.astype(bf16)
    split_ref[:, 0:256] = head
    split_ref[:, 256:512] = (table - head.astype(f32)).astype(bf16)

    def some_points(cluster, lane):
        index = order_ref[0:1, pl.ds(pl.multiple_of(cluster * PTS + lane, LANES), LANES)]
        k = lax.broadcasted_iota(jnp.int32, (256, LANES), 0)
        hot = jnp.where(k == (index & 255), 1.0, 0.0).astype(bf16)
        found = contract(split_ref[...], jnp.concatenate([hot, hot], axis=0), 1, 0)
        m = lax.broadcasted_iota(jnp.int32, (64, LANES), 0)
        here = m == (index >> 8)
        for part in range(4):
            rows = found[part * 64 : part * 64 + 64]
            out_ref[cluster, part : part + 1, lane : lane + LANES] = jnp.sum(
                jnp.where(here, rows, 0.0), axis=0, keepdims=True
            )

    def turn(number, carry):
        for inner in range(PICK_TURN):
            for lane in range(0, PTS, LANES):
                some_points(number * PICK_TURN + inner, lane)
        return carry

    lax.fori_loop(0, CL_DEV // PICK_TURN, turn, 0)


def pick(order, coords, weights):
    return pl.pallas_call(
        pick_kernel,
        out_shape=jax.ShapeDtypeStruct((CL_DEV, 4, PTS), f32),
        in_specs=[pl.BlockSpec(memory_space=pltpu.VMEM)] * 3,
        out_specs=pl.BlockSpec(memory_space=pltpu.VMEM),
        scratch_shapes=[pltpu.VMEM((256, 256), f32), pltpu.VMEM((256, 512), bf16)],
        compiler_params=pltpu.CompilerParams(vmem_limit_bytes=32 << 20),
        cost_estimate=pl.CostEstimate(
            flops=5_000_000_000, bytes_accessed=600_000, transcendentals=0
        ),
        name="pick",
    )(order, coords, weights)


def plan_kernel(row_ref, col_ref, slots_ref, rank_ref, wanted_ref, places_ref):
    count = rank_ref.shape[1]
    square = (count, count)
    row_owner, col_owner = row_ref[...].astype(f32), col_ref[...].astype(f32)
    row_slot, col_slot = slots_ref[0:1, :].astype(f32), slots_ref[1:2, :].astype(f32)
    rank = rank_ref[...].astype(f32)
    down = lax.broadcasted_iota(jnp.int32, square, 0)
    along = lax.broadcasted_iota(jnp.int32, square, 1)
    eye = down == along
    number = along.astype(f32)
    number_down = down.astype(f32)

    def column(row):
        return jnp.sum(jnp.where(eye, row, 0.0), axis=1, keepdims=True)

    def product(a, b):
        return jnp.where(contract(a, b, 1, 0) > 0.5, 1.0, 0.0).astype(bf16)

    same_row = jnp.where((column(row_owner) == row_owner) & ~eye, 1.0, 0.0)
    same_col = jnp.where((column(col_owner) == col_owner) & ~eye, 1.0, 0.0)
    either = (same_row + same_col).astype(bf16)
    same_row, same_col = same_row.astype(bf16), same_col.astype(bf16)
    steps = contract(same_row, same_col, 1, 0) + contract(same_col, same_row, 1, 0)
    alike = jnp.where(eye | (steps > 0.5), 1.0, 0.0).astype(bf16)
    for _ in range(4):
        alike = product(alike, alike)
    other = product(alike, either)
    far = float(2 * count)
    least = jnp.min(jnp.where(alike.astype(f32) > 0.5, number, far), axis=1, keepdims=True)
    least_other = jnp.min(jnp.where(other.astype(f32) > 0.5, number, far), axis=1, keepdims=True)
    first = jnp.where(least < least_other, 1.0, 0.0)
    size = jnp.sum(first, axis=0, keepdims=True)
    flip = size < count / 2
    first = jnp.where(flip, 1.0 - first, first)
    size = jnp.where(flip, count - size, size)
    first_row = jnp.sum(jnp.where(eye, first, 0.0), axis=0, keepdims=True)
    before = jnp.sum(jnp.where(along < down, first_row, 0.0), axis=1, keepdims=True)
    before_other = jnp.sum(jnp.where(along < down, 1.0 - first_row, 0.0), axis=1, keepdims=True)
    position = jnp.where(first > 0.5, before, size + before_other)
    hit = position == number

    def ordered(values):
        return jnp.sum(jnp.where(hit, values, 0.0), axis=0, keepdims=True)

    places = [
        ordered(number_down),
        ordered(column(row_owner * 2.0)),
        ordered(column(col_owner * 2.0 + 1.0)),
        ordered(column(rank)),
        ordered(1.0 - first),
    ]
    for line, value in enumerate(places):
        places_ref[line : line + 1, :] = value.astype(jnp.int32)
    places_ref[5:8, :] = jnp.zeros((3, count), jnp.int32)
    lane = lax.broadcasted_iota(jnp.int32, wanted_ref.shape, 1)
    wanted = jnp.zeros(wanted_ref.shape, f32)
    for phase in range(2):
        turn = first_row > 0.5 if phase == 0 else first_row < 0.5
        for side, (owner, slot) in enumerate(((row_owner, row_slot), (col_owner, col_slot))):
            value = jnp.sum(
                jnp.where((owner == number_down) & turn, slot, 0.0), axis=1, keepdims=True
            )
            wanted = jnp.where(lane == phase * 2 + side, value, wanted)
    wanted_ref[...] = wanted.astype(jnp.int32)


def plan(row_owner, col_owner, slots, rank, members):
    count = rank.shape[1]
    return pl.pallas_call(
        plan_kernel,
        out_shape=[
            jax.ShapeDtypeStruct((members, 128), jnp.int32),
            jax.ShapeDtypeStruct((8, count), jnp.int32),
        ],
        in_specs=[pl.BlockSpec(memory_space=pltpu.VMEM)] * 4,
        out_specs=[pl.BlockSpec(memory_space=pltpu.VMEM)] * 2,
        name="plan",
    )(row_owner, col_owner, slots, rank)


def reply_kernel(phase, wanted_ref, points_ref, out_ref, sem):
    for member in range(out_ref.shape[0]):
        for side in range(2):
            pltpu.make_async_copy(
                points_ref.at[wanted_ref[member, phase * 2 + side]],
                out_ref.at[member, side],
                sem,
            ).start()
    pltpu.make_async_copy(out_ref, out_ref, sem).wait()


def reply(phase, wanted, points):
    members = wanted.shape[0]
    return pl.pallas_call(
        functools.partial(reply_kernel, phase),
        in_specs=[
            pl.BlockSpec(memory_space=pltpu.SMEM),
            pl.BlockSpec(memory_space=pltpu.VMEM),
        ],
        out_specs=pl.BlockSpec(memory_space=pltpu.HBM),
        out_shape=jax.ShapeDtypeStruct((members, 2, 4, PTS), f32),
        scratch_shapes=[pltpu.SemaphoreType.DMA],
        cost_estimate=pl.CostEstimate(flops=0, bytes_accessed=4_000_000, transcendentals=0),
        name="reply",
    )(wanted, points)


def split3(value):
    first = value.astype(bf16).astype(f32)
    rest = value - first
    second = rest.astype(bf16).astype(f32)
    return first, second, rest - second


def distance_operands(rows, cols):
    line = lax.broadcasted_iota(jnp.int32, (4, PTS), 0)
    row_square = rows[0:1] * rows[0:1] + rows[1:2] * rows[1:2] + rows[2:3] * rows[2:3]
    left = jnp.where(line < 3, rows, row_square)
    inverse = 1.0 / (cols[3:4] * cols[3:4])
    col_square = cols[0:1] * cols[0:1] + cols[1:2] * cols[1:2] + cols[2:3] * cols[2:3]
    right = jnp.where(line < 3, cols * (-2.0 * inverse), inverse)
    l1, l2, l3 = split3(left)
    r1, r2, r3 = split3(right)
    c1, c2, c3 = split3((col_square + softening) * inverse)
    ones = jnp.ones((4, PTS), f32)
    zero = jnp.zeros((4, PTS), f32)
    last = jnp.where(line == 0, c1, jnp.where(line == 1, c2, jnp.where(line == 2, c3, 0.0)))
    left = jnp.concatenate([l1, l1, l2, l1, l2, l3, ones, zero], axis=0).astype(bf16)
    right = jnp.concatenate([r1, r2, r1, r3, r2, r1, last, zero], axis=0).astype(bf16)
    return left, right


def pair_kernel(first, number, phases, places, *refs):
    replies = refs[:phases]
    sketch_ref = refs[phases]
    range_ref, co_ref, turned_ref, left_ref, right_ref = refs[-5:]
    p = pl.program_id(0)

    def prepare(pair, slot):
        row_at, col_at = places[1, pair], places[2, pair]
        rows, cols = replies[0][row_at], replies[0][col_at]
        if phases > 1:
            early = places[4, pair] == 0
            rows = jnp.where(early, rows, replies[1][row_at])
            cols = jnp.where(early, cols, replies[1][col_at])
        left, right = distance_operands(rows, cols)
        left_ref[slot] = left
        right_ref[slot] = right.T

    @pl.when(p == 0)
    def _():
        prepare(first, 0)

    slot = lax.rem(p, 2)
    limit = places[3, first + p] * BLK
    test = sketch_ref[0]
    active = lax.broadcasted_iota(jnp.int32, (1, RK), 1) < limit
    masked = jnp.where(active, test, jnp.zeros_like(test)).T
    block = lax.rsqrt(contract(right_ref[slot], left_ref[slot], 1, 0)).astype(bf16)
    prepare(first + jnp.minimum(p + 1, number - 1), 1 - slot)
    ranged = contract(masked, block, 1, 0).astype(bf16)
    range_ref[0] = ranged.T
    turned_ref[...] = block.T
    co_ref[0] = (contract(ranged, turned_ref[...], 1, 0) * (1.0 / math.sqrt(PTS))).astype(bf16)


def pair_products(first, number, places, replies, sketch, old):
    count = sketch.shape[0]

    def own(p, places):
        return (places[0, first + p], 0, 0)

    pair_specs = [pl.BlockSpec((1, PTS, RK), own), pl.BlockSpec((1, RK, PTS), own)]
    operands = [places] + list(replies) + [sketch] + list(old)
    return pl.pallas_call(
        functools.partial(pair_kernel, first, number, len(replies)),
        grid_spec=pltpu.PrefetchScalarGridSpec(
            num_scalar_prefetch=1,
            grid=(number,),
            in_specs=[pl.BlockSpec(memory_space=pltpu.VMEM) for _ in replies]
            + pair_specs[:1]
            + [pl.BlockSpec(memory_space=pl.ANY) for _ in old],
            out_specs=pair_specs,
            scratch_shapes=[
                pltpu.VMEM((PTS, PTS), bf16),
                pltpu.VMEM((2, 32, PTS), bf16),
                pltpu.VMEM((2, PTS, 32), bf16),
            ],
        ),
        out_shape=[
            jax.ShapeDtypeStruct((count, PTS, RK), bf16),
            jax.ShapeDtypeStruct((count, RK, PTS), bf16),
        ],
        input_output_aliases={len(operands) - 2: 0, len(operands) - 1: 1} if old else {},
        compiler_params=pltpu.CompilerParams(vmem_limit_bytes=48 << 20),
        cost_estimate=pl.CostEstimate(
            flops=number * 6 * PTS * PTS * 256, bytes_accessed=number * 800_000, transcendentals=0
        ),
        name="pairs",
    )(*operands)


def shards(
    panel_coords, panel_weights, panel_order, row_owner, col_owner, pair_slots, rank_blocks, sketch
):
    members = lax.axis_size("dev")
    count = rank_blocks.shape[0]
    wanted, places = plan(
        row_owner.reshape(1, count),
        col_owner.reshape(1, count),
        pair_slots.T,
        rank_blocks.reshape(1, count),
        members,
    )
    asked = lax.all_to_all(wanted, "dev", split_axis=0, concat_axis=0, tiled=True)
    points = pick(panel_order, panel_coords, panel_weights.reshape(128, 128))
    replies = []
    for phase in range(2):
        found = reply(phase, asked, points)
        got = lax.all_to_all(found, "dev", split_axis=0, concat_axis=0, tiled=True)
        replies.append(got.reshape(members * 2, 4, PTS))
    half = count // 2
    early = pair_products(0, half, places, replies[:1], sketch, ())
    return tuple(pair_products(half, count - half, places, replies, sketch, early))


def solution(mesh):
    in_specs = (
        P(None, ("leaf", "dev")),
        P(("leaf", "dev")),
        P(("leaf", "dev"), None),
        P(("leaf", "dev"), None),
        P(("leaf", "dev"), None),
        P(("leaf", "dev"), None),
        P(("leaf", "dev")),
        P(("leaf", "dev"), None, None),
    )
    out_specs = (P(("leaf", "dev"), None, None), P(("leaf", "dev"), None, None))
    return jax.shard_map(shards, mesh=mesh, in_specs=in_specs, out_specs=out_specs, check_vma=False)
```

```python
import functools
import math

import jax
import jax.numpy as jnp
from jax import lax
from jax.experimental import pallas as pl
from jax.experimental.pallas import tpu as pltpu
from jax.sharding import PartitionSpec as P

PTS = 1024
RK = 128
BLK = 32
CL_DEV = 16
CHUNK = 256

softening = 0.01
bf16 = jnp.bfloat16
f32 = jnp.float32


def contract(a, b, dim_a, dim_b):
    return lax.dot_general(a, b, (((dim_a,), (dim_b,)), ((), ())), preferred_element_type=f32)

PICK_TURN = 2
LANES = 256


def pick_kernel(
    asked_ref,
    order_hbm,
    coords_hbm,
    weights_hbm,
    out_ref,
    found_ref,
    order_ref,
    coords_ref,
    weights_ref,
    asked_smem,
    table_ref,
    split_ref,
    sems,
    found_sem,
):
    fetches = [
        pltpu.make_async_copy(source, target, sems.at[i])
        for i, (source, target) in enumerate(
            (
                (coords_hbm, coords_ref),
                (weights_hbm, weights_ref),
                (order_hbm, order_ref),
                (asked_ref, asked_smem),
            )
        )
    ]
    for fetch in fetches:
        fetch.start()
    fetches[0].wait()
    for part in range(3):
        for m in range(64):
            table_ref[part * 64 + m : part * 64 + m + 1, :] = coords_ref[
                part : part + 1, m * 256 : m * 256 + 256
            ]
    fetches[1].wait()
    for half in range(2):
        table_ref[192:256, half * 128 : half * 128 + 128] = weights_ref[
            pl.ds(half, 64, stride=2), :
        ]
    table = table_ref[...]
    head = table.astype(bf16)
    split_ref[:, 0:256] = head
    split_ref[:, 256:512] = (table - head.astype(f32)).astype(bf16)

    fetches[2].wait()

    def some_points(cluster, lane):
        index = order_ref[0:1, pl.ds(pl.multiple_of(cluster * PTS + lane, LANES), LANES)]
        k = lax.broadcasted_iota(jnp.int32, (256, LANES), 0)
        hot = jnp.where(k == (index & 255), 1.0, 0.0).astype(bf16)
        found = contract(split_ref[...], jnp.concatenate([hot, hot], axis=0), 1, 0)
        m = lax.broadcasted_iota(jnp.int32, (64, LANES), 0)
        here = m == (index >> 8)
        for part in range(4):
            rows = found[part * 64 : part * 64 + 64]
            out_ref[cluster, part : part + 1, lane : lane + LANES] = jnp.sum(
                jnp.where(here, rows, 0.0), axis=0, keepdims=True
            )

    def turn(number, carry):
        for inner in range(PICK_TURN):
            for lane in range(0, PTS, LANES):
                some_points(number * PICK_TURN + inner, lane)
        return carry

    lax.fori_loop(0, CL_DEV // PICK_TURN, turn, 0)
    fetches[3].wait()
    send_found(0, asked_smem, out_ref, found_ref, found_sem)


def send_found(phase, asked_smem, points_ref, found_ref, sem):
    for member in range(found_ref.shape[0]):
        for side in range(2):
            pltpu.make_async_copy(
                points_ref.at[asked_smem[member, phase * 2 + side]],
                found_ref.at[member, side],
                sem,
            ).start()
    pltpu.make_async_copy(found_ref, found_ref, sem).wait()


def pick(asked, order, coords, weights):
    members = asked.shape[0]
    return pl.pallas_call(
        pick_kernel,
        out_shape=[
            jax.ShapeDtypeStruct((CL_DEV, 4, PTS), f32),
            jax.ShapeDtypeStruct((members, 2, 4, PTS), f32),
        ],
        in_specs=[pl.BlockSpec(memory_space=pltpu.VMEM)]
        + [pl.BlockSpec(memory_space=pltpu.HBM)] * 3,
        out_specs=[
            pl.BlockSpec(memory_space=pltpu.VMEM),
            pl.BlockSpec(memory_space=pltpu.HBM),
        ],
        scratch_shapes=[
            pltpu.VMEM(order.shape, jnp.int32),
            pltpu.VMEM(coords.shape, f32),
            pltpu.VMEM(weights.shape, f32),
            pltpu.SMEM(asked.shape, jnp.int32),
            pltpu.VMEM((256, 256), f32),
            pltpu.VMEM((256, 512), bf16),
            pltpu.SemaphoreType.DMA((4,)),
            pltpu.SemaphoreType.DMA,
        ],
        compiler_params=pltpu.CompilerParams(vmem_limit_bytes=56 << 20),
        cost_estimate=pl.CostEstimate(
            flops=5_000_000_000, bytes_accessed=4_000_000, transcendentals=0
        ),
        name="pick",
    )(asked, order, coords, weights)


def plan_kernel(row_ref, col_ref, slots_ref, rank_ref, wanted_ref, places_ref):
    count = rank_ref.shape[1]
    square = (count, count)
    row_owner, col_owner = row_ref[...].astype(f32), col_ref[...].astype(f32)
    row_slot, col_slot = slots_ref[0:1, :].astype(f32), slots_ref[1:2, :].astype(f32)
    rank = rank_ref[...].astype(f32)
    down = lax.broadcasted_iota(jnp.int32, square, 0)
    along = lax.broadcasted_iota(jnp.int32, square, 1)
    eye = down == along
    number = along.astype(f32)
    number_down = down.astype(f32)

    def column(row):
        return jnp.sum(jnp.where(eye, row, 0.0), axis=1, keepdims=True)

    def product(a, b):
        return jnp.where(contract(a, b, 1, 0) > 0.5, 1.0, 0.0).astype(bf16)

    same_row = jnp.where((column(row_owner) == row_owner) & ~eye, 1.0, 0.0)
    same_col = jnp.where((column(col_owner) == col_owner) & ~eye, 1.0, 0.0)
    either = (same_row + same_col).astype(bf16)
    same_row, same_col = same_row.astype(bf16), same_col.astype(bf16)
    steps = contract(same_row, same_col, 1, 0) + contract(same_col, same_row, 1, 0)
    alike = jnp.where(eye | (steps > 0.5), 1.0, 0.0).astype(bf16)
    for _ in range(4):
        alike = product(alike, alike)
    other = product(alike, either)
    far = float(2 * count)
    least = jnp.min(jnp.where(alike.astype(f32) > 0.5, number, far), axis=1, keepdims=True)
    least_other = jnp.min(jnp.where(other.astype(f32) > 0.5, number, far), axis=1, keepdims=True)
    first = jnp.where(least < least_other, 1.0, 0.0)
    size = jnp.sum(first, axis=0, keepdims=True)
    flip = size < count / 2
    first = jnp.where(flip, 1.0 - first, first)
    size = jnp.where(flip, count - size, size)
    first_row = jnp.sum(jnp.where(eye, first, 0.0), axis=0, keepdims=True)
    before = jnp.sum(jnp.where(along < down, first_row, 0.0), axis=1, keepdims=True)
    before_other = jnp.sum(jnp.where(along < down, 1.0 - first_row, 0.0), axis=1, keepdims=True)
    position = jnp.where(first > 0.5, before, size + before_other)
    hit = position == number

    def ordered(values):
        return jnp.sum(jnp.where(hit, values, 0.0), axis=0, keepdims=True)

    places = [
        ordered(number_down),
        ordered(column(row_owner * 2.0)),
        ordered(column(col_owner * 2.0 + 1.0)),
        ordered(column(rank)),
        ordered(1.0 - first),
    ]
    for line, value in enumerate(places):
        places_ref[line : line + 1, :] = value.astype(jnp.int32)
    places_ref[5:8, :] = jnp.zeros((3, count), jnp.int32)
    lane = lax.broadcasted_iota(jnp.int32, wanted_ref.shape, 1)
    wanted = jnp.zeros(wanted_ref.shape, f32)
    for phase in range(2):
        turn = first_row > 0.5 if phase == 0 else first_row < 0.5
        for side, (owner, slot) in enumerate(((row_owner, row_slot), (col_owner, col_slot))):
            value = jnp.sum(
                jnp.where((owner == number_down) & turn, slot, 0.0), axis=1, keepdims=True
            )
            wanted = jnp.where(lane == phase * 2 + side, value, wanted)
    wanted_ref[...] = wanted.astype(jnp.int32)


def plan(row_owner, col_owner, slots, rank, members):
    count = rank.shape[1]
    return pl.pallas_call(
        plan_kernel,
        out_shape=[
            jax.ShapeDtypeStruct((members, 128), jnp.int32),
            jax.ShapeDtypeStruct((8, count), jnp.int32),
        ],
        in_specs=[pl.BlockSpec(memory_space=pltpu.VMEM)] * 4,
        out_specs=[pl.BlockSpec(memory_space=pltpu.VMEM)] * 2,
        name="plan",
    )(row_owner, col_owner, slots, rank)


def reply_kernel(asked_ref, points_ref, found_ref, asked_smem, asked_sem, sem):
    fetch = pltpu.make_async_copy(asked_ref, asked_smem, asked_sem)
    fetch.start()
    fetch.wait()
    send_found(1, asked_smem, points_ref, found_ref, sem)


def reply(asked, points):
    return pl.pallas_call(
        reply_kernel,
        in_specs=[pl.BlockSpec(memory_space=pltpu.VMEM)] * 2,
        out_specs=pl.BlockSpec(memory_space=pltpu.HBM),
        out_shape=jax.ShapeDtypeStruct((asked.shape[0], 2, 4, PTS), f32),
        scratch_shapes=[
            pltpu.SMEM(asked.shape, jnp.int32),
            pltpu.SemaphoreType.DMA,
            pltpu.SemaphoreType.DMA,
        ],
        cost_estimate=pl.CostEstimate(flops=0, bytes_accessed=4_000_000, transcendentals=0),
        name="reply",
    )(asked, points)


def split3(value):
    first = value.astype(bf16).astype(f32)
    rest = value - first
    second = rest.astype(bf16).astype(f32)
    return first, second, rest - second


def distance_operands(rows, cols):
    line = lax.broadcasted_iota(jnp.int32, (4, PTS), 0)
    row_square = rows[0:1] * rows[0:1] + rows[1:2] * rows[1:2] + rows[2:3] * rows[2:3]
    left = jnp.where(line < 3, rows, row_square)
    inverse = 1.0 / (cols[3:4] * cols[3:4])
    col_square = cols[0:1] * cols[0:1] + cols[1:2] * cols[1:2] + cols[2:3] * cols[2:3]
    right = jnp.where(line < 3, cols * (-2.0 * inverse), inverse)
    l1, l2, l3 = split3(left)
    r1, r2, r3 = split3(right)
    c1, c2, c3 = split3((col_square + softening) * inverse)
    ones = jnp.ones((4, PTS), f32)
    zero = jnp.zeros((4, PTS), f32)
    last = jnp.where(line == 0, c1, jnp.where(line == 1, c2, jnp.where(line == 2, c3, 0.0)))
    left = jnp.concatenate([l1, l1, l2, l1, l2, l3, ones, zero], axis=0).astype(bf16)
    right = jnp.concatenate([r1, r2, r1, r3, r2, r1, last, zero], axis=0).astype(bf16)
    return left, right


def pair_kernel(first, steps, phases, places, *refs):
    replies = refs[:phases]
    sketches = refs[phases : phases + 2]
    range_ref, co_ref = refs[-12:-10]
    turned, ranged = refs[-10:-8], refs[-8:-6]
    left_ref, right_ref, range_out, co_out = refs[-6:-2]
    range_sem, co_sem = refs[-2:]
    p = pl.program_id(0)
    slot = lax.rem(p, 2)
    scale = 1.0 / math.sqrt(PTS)

    def prepare(pair, side):
        row_at, col_at = places[1, pair], places[2, pair]
        rows, cols = replies[0][row_at], replies[0][col_at]
        if phases > 1:
            early = places[4, pair] == 0
            rows = jnp.where(early, rows, replies[1][row_at])
            cols = jnp.where(early, cols, replies[1][col_at])
        left, right = distance_operands(rows, cols)
        left_ref[side] = left
        right_ref[side] = right.T

    def send_range(step, side):
        at = lax.rem(step, 2)
        return pltpu.make_async_copy(
            range_out.at[at, side],
            range_ref.at[places[0, first + 2 * step + side]],
            range_sem.at[at, side],
        )

    def send_co(step, side):
        at = lax.rem(step, 2)
        return pltpu.make_async_copy(
            co_out.at[at, side],
            co_ref.at[places[0, first + 2 * step - 1 + side]],
            co_sem.at[at, side],
        )

    @pl.when(p == 0)
    def _():
        for side in range(2):
            prepare(first + side, side)

    @pl.when(p >= 2)
    def _():
        for side in range(2):
            send_range(p - 2, side).wait()
        send_co(p - 2, 1).wait()

    @pl.when(p >= 3)
    def _():
        send_co(p - 2, 0).wait()

    following = jnp.minimum(p + 1, steps - 1)
    for side in range(2):
        other = 1 - side
        left, right = left_ref[side], right_ref[side]
        limit = places[3, first + 2 * p + side] * BLK
        test = sketches[side][0]
        active = lax.broadcasted_iota(jnp.int32, (1, RK), 1) < limit
        masked = jnp.where(active, test, jnp.zeros_like(test)).T
        for start in range(0, PTS, CHUNK):
            part = slice(start, start + CHUNK)
            block = lax.rsqrt(contract(right, left[:, part], 1, 0)).astype(bf16)
            product = contract(ranged[other][...], turned[other][:, part], 1, 0)
            co_out[slot, side, :, part] = (product * scale).astype(bf16)
            if start == 0:
                prepare(first + 2 * following + side, side)
            some = contract(masked, block, 1, 0).astype(bf16)
            range_out[slot, side, part, :] = some.T
            ranged[side][:, part] = some
            turned[side][part, :] = block.T

    for side in range(2):
        send_range(p, side).start()
    send_co(p, 1).start()

    @pl.when(p >= 1)
    def _():
        send_co(p, 0).start()

    @pl.when(p == steps - 1)
    def _():
        send_co(p - 1, 0).wait()
        product = contract(ranged[1][...], turned[1][...], 1, 0)
        co_out[1 - slot, 0] = (product * scale).astype(bf16)
        send_co(p + 1, 0).start()
        for side in range(2):
            send_range(p - 1, side).wait()
            send_range(p, side).wait()
            send_co(p, side).wait()
        send_co(p - 1, 1).wait()
        send_co(p + 1, 0).wait()


def pair_products(first, number, places, replies, sketch, old):
    count = sketch.shape[0]
    steps = number // 2
    assert number == 2 * steps and steps >= 3

    def own(side):
        return lambda p, places: (places[0, first + 2 * p + side], 0, 0)

    operands = [places] + list(replies) + [sketch, sketch] + list(old)
    return pl.pallas_call(
        functools.partial(pair_kernel, first, steps, len(replies)),
        grid_spec=pltpu.PrefetchScalarGridSpec(
            num_scalar_prefetch=1,
            grid=(steps,),
            in_specs=[pl.BlockSpec(memory_space=pltpu.VMEM) for _ in replies]
            + [pl.BlockSpec((1, PTS, RK), own(side)) for side in range(2)]
            + [pl.BlockSpec(memory_space=pl.ANY) for _ in old],
            out_specs=[pl.BlockSpec(memory_space=pl.ANY)] * 2,
            scratch_shapes=[pltpu.VMEM((PTS, PTS), bf16)] * 2
            + [pltpu.VMEM((RK, PTS), bf16)] * 2
            + [
                pltpu.VMEM((2, 32, PTS), bf16),
                pltpu.VMEM((2, PTS, 32), bf16),
                pltpu.VMEM((2, 2, PTS, RK), bf16),
                pltpu.VMEM((2, 2, RK, PTS), bf16),
                pltpu.SemaphoreType.DMA((2, 2)),
                pltpu.SemaphoreType.DMA((2, 2)),
            ],
        ),
        out_shape=[
            jax.ShapeDtypeStruct((count, PTS, RK), bf16),
            jax.ShapeDtypeStruct((count, RK, PTS), bf16),
        ],
        input_output_aliases={len(operands) - 2: 0, len(operands) - 1: 1} if old else {},
        compiler_params=pltpu.CompilerParams(vmem_limit_bytes=48 << 20),
        cost_estimate=pl.CostEstimate(
            flops=number * 6 * PTS * PTS * 256, bytes_accessed=number * 800_000, transcendentals=0
        ),
        name="pairs",
    )(*operands)


def shards(
    panel_coords, panel_weights, panel_order, row_owner, col_owner, pair_slots, rank_blocks, sketch
):
    members = lax.axis_size("dev")
    count = rank_blocks.shape[0]
    wanted, places = plan(
        row_owner.reshape(1, count),
        col_owner.reshape(1, count),
        pair_slots.T,
        rank_blocks.reshape(1, count),
        members,
    )
    asked = lax.all_to_all(wanted, "dev", split_axis=0, concat_axis=0, tiled=True)
    points, found = pick(asked, panel_order, panel_coords, panel_weights.reshape(128, 128))
    replies = []
    for found in (found, reply(asked, points)):
        got = lax.all_to_all(found, "dev", split_axis=0, concat_axis=0, tiled=True)
        replies.append(got.reshape(members * 2, 4, PTS))
    half = count // 2
    early = pair_products(0, half, places, replies[:1], sketch, ())
    return tuple(pair_products(half, count - half, places, replies, sketch, early))


def solution(mesh):
    in_specs = (
        P(None, ("leaf", "dev")),
        P(("leaf", "dev")),
        P(("leaf", "dev"), None),
        P(("leaf", "dev"), None),
        P(("leaf", "dev"), None),
        P(("leaf", "dev"), None),
        P(("leaf", "dev")),
        P(("leaf", "dev"), None, None),
    )
    out_specs = (P(("leaf", "dev"), None, None), P(("leaf", "dev"), None, None))
    return jax.shard_map(shards, mesh=mesh, in_specs=in_specs, out_specs=out_specs, check_vma=False)
```

```python
import functools
import math

import jax
import jax.numpy as jnp
from jax import lax
from jax.experimental import pallas as pl
from jax.experimental.pallas import tpu as pltpu
from jax.sharding import PartitionSpec as P

PTS = 1024
RK = 128
BLK = 32
CL_DEV = 16
CHUNK = 256

softening = 0.01
bf16 = jnp.bfloat16
f32 = jnp.float32


def contract(a, b, dim_a, dim_b):
    return lax.dot_general(a, b, (((dim_a,), (dim_b,)), ((), ())), preferred_element_type=f32)

PICK_TURN = 2
LANES = 256


def pick_kernel(order_ref, coords_ref, weights_ref, out_ref, table_ref, split_ref):
    for part in range(3):
        for m in range(64):
            table_ref[part * 64 + m : part * 64 + m + 1, :] = coords_ref[
                part : part + 1, m * 256 : m * 256 + 256
            ]
    for half in range(2):
        table_ref[192:256, half * 128 : half * 128 + 128] = weights_ref[
            pl.ds(half, 64, stride=2), :
        ]
    table = table_ref[...]
    head = table.astype(bf16)
    split_ref[:, 0:256] = head
    split_ref[:, 256:512] = (table - head.astype(f32)).astype(bf16)

    def some_points(cluster, lane):
        index = order_ref[0:1, pl.ds(pl.multiple_of(cluster * PTS + lane, LANES), LANES)]
        k = lax.broadcasted_iota(jnp.int32, (256, LANES), 0).astype(f32).astype(bf16)
        low = (index & 255).astype(f32).astype(bf16)
        hot = jnp.where(k == low, jnp.ones((), bf16), jnp.zeros((), bf16))
        found = contract(split_ref[...], jnp.concatenate([hot, hot], axis=0), 1, 0)
        m = lax.broadcasted_iota(jnp.int32, (64, LANES), 0)
        here = m == (index >> 8)
        for part in range(4):
            rows = found[part * 64 : part * 64 + 64]
            out_ref[cluster, part : part + 1, lane : lane + LANES] = jnp.sum(
                jnp.where(here, rows, 0.0), axis=0, keepdims=True
            )

    def turn(number, carry):
        for inner in range(PICK_TURN):
            for lane in range(0, PTS, LANES):
                some_points(number * PICK_TURN + inner, lane)
        return carry

    lax.fori_loop(0, CL_DEV // PICK_TURN, turn, 0)


def pick(order, coords, weights):
    return pl.pallas_call(
        pick_kernel,
        out_shape=jax.ShapeDtypeStruct((CL_DEV, 4, PTS), f32),
        in_specs=[pl.BlockSpec(memory_space=pltpu.VMEM)] * 3,
        out_specs=pl.BlockSpec(memory_space=pltpu.VMEM),
        scratch_shapes=[pltpu.VMEM((256, 256), f32), pltpu.VMEM((256, 512), bf16)],
        compiler_params=pltpu.CompilerParams(vmem_limit_bytes=32 << 20),
        cost_estimate=pl.CostEstimate(
            flops=5_000_000_000, bytes_accessed=600_000, transcendentals=0
        ),
        name="pick",
    )(order, coords, weights)


def plan_kernel(row_ref, col_ref, slots_ref, rank_ref, wanted_ref, places_ref):
    count = rank_ref.shape[1]
    square = (count, count)
    row_owner, col_owner = row_ref[...].astype(f32), col_ref[...].astype(f32)
    row_slot, col_slot = slots_ref[0:1, :].astype(f32), slots_ref[1:2, :].astype(f32)
    rank = rank_ref[...].astype(f32)
    down = lax.broadcasted_iota(jnp.int32, square, 0)
    along = lax.broadcasted_iota(jnp.int32, square, 1)
    eye = down == along
    number = along.astype(f32)
    number_down = down.astype(f32)

    def column(row):
        return jnp.sum(jnp.where(eye, row, 0.0), axis=1, keepdims=True)

    def product(a, b):
        return jnp.where(contract(a, b, 1, 0) > 0.5, 1.0, 0.0).astype(bf16)

    same_row = jnp.where((column(row_owner) == row_owner) & ~eye, 1.0, 0.0)
    same_col = jnp.where((column(col_owner) == col_owner) & ~eye, 1.0, 0.0)
    either = (same_row + same_col).astype(bf16)
    same_row, same_col = same_row.astype(bf16), same_col.astype(bf16)
    steps = contract(same_row, same_col, 1, 0) + contract(same_col, same_row, 1, 0)
    alike = jnp.where(eye | (steps > 0.5), 1.0, 0.0).astype(bf16)
    for _ in range(4):
        alike = product(alike, alike)
    other = product(alike, either)
    far = float(2 * count)
    least = jnp.min(jnp.where(alike.astype(f32) > 0.5, number, far), axis=1, keepdims=True)
    least_other = jnp.min(jnp.where(other.astype(f32) > 0.5, number, far), axis=1, keepdims=True)
    first = jnp.where(least < least_other, 1.0, 0.0)
    size = jnp.sum(first, axis=0, keepdims=True)
    flip = size < count / 2
    first = jnp.where(flip, 1.0 - first, first)
    size = jnp.where(flip, count - size, size)
    first_row = jnp.sum(jnp.where(eye, first, 0.0), axis=0, keepdims=True)
    before = jnp.sum(jnp.where(along < down, first_row, 0.0), axis=1, keepdims=True)
    before_other = jnp.sum(jnp.where(along < down, 1.0 - first_row, 0.0), axis=1, keepdims=True)
    position = jnp.where(first > 0.5, before, size + before_other)
    hit = position == number

    def ordered(values):
        return jnp.sum(jnp.where(hit, values, 0.0), axis=0, keepdims=True)

    places = [
        ordered(number_down),
        ordered(column(row_owner * 2.0)),
        ordered(column(col_owner * 2.0 + 1.0)),
        ordered(column(rank)),
        ordered(1.0 - first),
    ]
    for line, value in enumerate(places):
        places_ref[line : line + 1, :] = value.astype(jnp.int32)
    places_ref[5:8, :] = jnp.zeros((3, count), jnp.int32)
    lane = lax.broadcasted_iota(jnp.int32, wanted_ref.shape, 1)
    wanted = jnp.zeros(wanted_ref.shape, f32)
    for phase in range(2):
        turn = first_row > 0.5 if phase == 0 else first_row < 0.5
        for side, (owner, slot) in enumerate(((row_owner, row_slot), (col_owner, col_slot))):
            value = jnp.sum(
                jnp.where((owner == number_down) & turn, slot, 0.0), axis=1, keepdims=True
            )
            wanted = jnp.where(lane == phase * 2 + side, value, wanted)
    wanted_ref[...] = wanted.astype(jnp.int32)


def plan(row_owner, col_owner, slots, rank, members):
    count = rank.shape[1]
    return pl.pallas_call(
        plan_kernel,
        out_shape=[
            jax.ShapeDtypeStruct((members, 128), jnp.int32),
            jax.ShapeDtypeStruct((8, count), jnp.int32),
        ],
        in_specs=[pl.BlockSpec(memory_space=pltpu.VMEM)] * 4,
        out_specs=[pl.BlockSpec(memory_space=pltpu.VMEM)] * 2,
        name="plan",
    )(row_owner, col_owner, slots, rank)


def reply_kernel(phase, asked_ref, points_ref, found_ref, asked_smem, asked_sem, sem):
    fetch = pltpu.make_async_copy(asked_ref, asked_smem, asked_sem)
    fetch.start()
    fetch.wait()
    for member in range(found_ref.shape[0]):
        for side in range(2):
            pltpu.make_async_copy(
                points_ref.at[asked_smem[member, phase * 2 + side]],
                found_ref.at[member, side],
                sem,
            ).start()
    pltpu.make_async_copy(found_ref, found_ref, sem).wait()


def reply(phase, asked, points):
    return pl.pallas_call(
        functools.partial(reply_kernel, phase),
        in_specs=[pl.BlockSpec(memory_space=pl.ANY), pl.BlockSpec(memory_space=pltpu.VMEM)],
        out_specs=pl.BlockSpec(memory_space=pltpu.HBM),
        out_shape=jax.ShapeDtypeStruct((asked.shape[0], 2, 4, PTS), f32),
        scratch_shapes=[
            pltpu.SMEM(asked.shape, jnp.int32),
            pltpu.SemaphoreType.DMA,
            pltpu.SemaphoreType.DMA,
        ],
        cost_estimate=pl.CostEstimate(flops=0, bytes_accessed=4_000_000, transcendentals=0),
        name="reply",
    )(asked, points)


def split3(value):
    first = value.astype(bf16).astype(f32)
    rest = value - first
    second = rest.astype(bf16).astype(f32)
    return first, second, rest - second


def distance_operands(rows, cols):
    line = lax.broadcasted_iota(jnp.int32, (4, PTS), 0)
    row_square = rows[0:1] * rows[0:1] + rows[1:2] * rows[1:2] + rows[2:3] * rows[2:3]
    left = jnp.where(line < 3, rows, row_square)
    inverse = 1.0 / (cols[3:4] * cols[3:4])
    col_square = cols[0:1] * cols[0:1] + cols[1:2] * cols[1:2] + cols[2:3] * cols[2:3]
    right = jnp.where(line < 3, cols * (-2.0 * inverse), inverse)
    l1, l2, l3 = split3(left)
    r1, r2, r3 = split3(right)
    c1, c2, c3 = split3((col_square + softening) * inverse)
    ones = jnp.ones((4, PTS), f32)
    zero = jnp.zeros((4, PTS), f32)
    last = jnp.where(line == 0, c1, jnp.where(line == 1, c2, jnp.where(line == 2, c3, 0.0)))
    left = jnp.concatenate([l1, l1, l2, l1, l2, l3, ones, zero], axis=0).astype(bf16)
    right = jnp.concatenate([r1, r2, r1, r3, r2, r1, last, zero], axis=0).astype(bf16)
    return left, right


def pair_kernel(first, steps, phases, places, *refs):
    replies = refs[:phases]
    sketches = refs[phases : phases + 2]
    range_ref, co_ref = refs[-12:-10]
    turned, ranged = refs[-10:-8], refs[-8:-6]
    left_ref, right_ref, range_out, co_out = refs[-6:-2]
    range_sem, co_sem = refs[-2:]
    p = pl.program_id(0)
    slot = lax.rem(p, 2)
    scale = 1.0 / math.sqrt(PTS)

    def prepare(pair, side):
        row_at, col_at = places[1, pair], places[2, pair]
        rows, cols = replies[0][row_at], replies[0][col_at]
        if phases > 1:
            early = places[4, pair] == 0
            rows = jnp.where(early, rows, replies[1][row_at])
            cols = jnp.where(early, cols, replies[1][col_at])
        left, right = distance_operands(rows, cols)
        left_ref[side] = left
        right_ref[side] = right.T

    def send_range(step, side):
        at = lax.rem(step, 2)
        return pltpu.make_async_copy(
            range_out.at[at, side],
            range_ref.at[places[0, first + 2 * step + side]],
            range_sem.at[at, side],
        )

    def send_co(step, side):
        at = lax.rem(step, 2)
        return pltpu.make_async_copy(
            co_out.at[at, side],
            co_ref.at[places[0, first + 2 * step - 1 + side]],
            co_sem.at[at, side],
        )

    @pl.when(p == 0)
    def _():
        for side in range(2):
            prepare(first + side, side)

    @pl.when(p >= 2)
    def _():
        for side in range(2):
            send_range(p - 2, side).wait()
        send_co(p - 2, 1).wait()

    @pl.when(p >= 3)
    def _():
        send_co(p - 2, 0).wait()

    following = jnp.minimum(p + 1, steps - 1)
    for side in range(2):
        other = 1 - side
        left, right = left_ref[side], right_ref[side]
        limit = places[3, first + 2 * p + side] * BLK
        test = sketches[side][0]
        active = lax.broadcasted_iota(jnp.int32, (1, RK), 1) < limit
        masked = jnp.where(active, test, jnp.zeros_like(test)).T
        for start in range(0, PTS, CHUNK):
            part = slice(start, start + CHUNK)
            block = lax.rsqrt(contract(right, left[:, part], 1, 0)).astype(bf16)
            product = contract(ranged[other][...], turned[other][:, part], 1, 0)
            co_out[slot, side, :, part] = (product * scale).astype(bf16)
            if start == 0:
                prepare(first + 2 * following + side, side)
            some = contract(masked, block, 1, 0).astype(bf16)
            range_out[slot, side, part, :] = some.T
            ranged[side][:, part] = some
            turned[side][part, :] = block.T

    for side in range(2):
        send_range(p, side).start()
    send_co(p, 1).start()

    @pl.when(p >= 1)
    def _():
        send_co(p, 0).start()

    @pl.when(p == steps - 1)
    def _():
        send_co(p - 1, 0).wait()
        product = contract(ranged[1][...], turned[1][...], 1, 0)
        co_out[1 - slot, 0] = (product * scale).astype(bf16)
        send_co(p + 1, 0).start()
        for side in range(2):
            send_range(p - 1, side).wait()
            send_range(p, side).wait()
            send_co(p, side).wait()
        send_co(p - 1, 1).wait()
        send_co(p + 1, 0).wait()


def pair_products(first, number, places, replies, sketch, old):
    count = sketch.shape[0]
    steps = number // 2
    assert number == 2 * steps and steps >= 3

    def own(side):
        return lambda p, places: (places[0, first + 2 * p + side], 0, 0)

    operands = [places] + list(replies) + [sketch, sketch] + list(old)
    return pl.pallas_call(
        functools.partial(pair_kernel, first, steps, len(replies)),
        grid_spec=pltpu.PrefetchScalarGridSpec(
            num_scalar_prefetch=1,
            grid=(steps,),
            in_specs=[pl.BlockSpec(memory_space=pltpu.VMEM) for _ in replies]
            + [pl.BlockSpec((1, PTS, RK), own(side)) for side in range(2)]
            + [pl.BlockSpec(memory_space=pl.ANY) for _ in old],
            out_specs=[pl.BlockSpec(memory_space=pl.ANY)] * 2,
            scratch_shapes=[pltpu.VMEM((PTS, PTS), bf16)] * 2
            + [pltpu.VMEM((RK, PTS), bf16)] * 2
            + [
                pltpu.VMEM((2, 32, PTS), bf16),
                pltpu.VMEM((2, PTS, 32), bf16),
                pltpu.VMEM((2, 2, PTS, RK), bf16),
                pltpu.VMEM((2, 2, RK, PTS), bf16),
                pltpu.SemaphoreType.DMA((2, 2)),
                pltpu.SemaphoreType.DMA((2, 2)),
            ],
        ),
        out_shape=[
            jax.ShapeDtypeStruct((count, PTS, RK), bf16),
            jax.ShapeDtypeStruct((count, RK, PTS), bf16),
        ],
        input_output_aliases={len(operands) - 2: 0, len(operands) - 1: 1} if old else {},
        compiler_params=pltpu.CompilerParams(vmem_limit_bytes=48 << 20),
        cost_estimate=pl.CostEstimate(
            flops=number * 6 * PTS * PTS * 256, bytes_accessed=number * 800_000, transcendentals=0
        ),
        name="pairs",
    )(*operands)


def shards(
    panel_coords, panel_weights, panel_order, row_owner, col_owner, pair_slots, rank_blocks, sketch
):
    members = lax.axis_size("dev")
    count = rank_blocks.shape[0]
    wanted, places = plan(
        row_owner.reshape(1, count),
        col_owner.reshape(1, count),
        pair_slots.T,
        rank_blocks.reshape(1, count),
        members,
    )
    asked = lax.all_to_all(wanted, "dev", split_axis=0, concat_axis=0, tiled=True)
    points = pick(panel_order, panel_coords, panel_weights.reshape(128, 128))
    replies = []
    for phase in range(2):
        found = reply(phase, asked, points)
        got = lax.all_to_all(found, "dev", split_axis=0, concat_axis=0, tiled=True)
        replies.append(got.reshape(members * 2, 4, PTS))
    half = count // 2
    early = pair_products(0, half, places, replies[:1], sketch, ())
    return tuple(pair_products(half, count - half, places, replies, sketch, early))


def solution(mesh):
    in_specs = (
        P(None, ("leaf", "dev")),
        P(("leaf", "dev")),
        P(("leaf", "dev"), None),
        P(("leaf", "dev"), None),
        P(("leaf", "dev"), None),
        P(("leaf", "dev"), None),
        P(("leaf", "dev")),
        P(("leaf", "dev"), None, None),
    )
    out_specs = (P(("leaf", "dev"), None, None), P(("leaf", "dev"), None, None))
    return jax.shard_map(shards, mesh=mesh, in_specs=in_specs, out_specs=out_specs, check_vma=False)
```

```python
import functools
import math

import jax
import jax.numpy as jnp
from jax import lax
from jax.experimental import pallas as pl
from jax.experimental.pallas import tpu as pltpu
from jax.sharding import PartitionSpec as P

PTS = 1024
RK = 128
BLK = 32
CL_DEV = 16
CHUNK = 256

softening = 0.01
bf16 = jnp.bfloat16
f32 = jnp.float32


def contract(a, b, dim_a, dim_b):
    return lax.dot_general(a, b, (((dim_a,), (dim_b,)), ((), ())), preferred_element_type=f32)

PICK_TURN = 8
LANES = 256


def pick_kernel(order_ref, coords_ref, weights_ref, out_ref, table_ref, split_ref):
    for part in range(3):
        for m in range(64):
            table_ref[part * 64 + m : part * 64 + m + 1, :] = coords_ref[
                part : part + 1, m * 256 : m * 256 + 256
            ]
    for half in range(2):
        table_ref[192:256, half * 128 : half * 128 + 128] = weights_ref[
            pl.ds(half, 64, stride=2), :
        ]
    table = table_ref[...]
    head = table.astype(bf16)
    split_ref[:, 0:256] = head
    split_ref[:, 256:512] = (table - head.astype(f32)).astype(bf16)

    def some_points(cluster, lane):
        index = order_ref[0:1, pl.ds(pl.multiple_of(cluster * PTS + lane, LANES), LANES)]
        k = lax.broadcasted_iota(jnp.int32, (256, LANES), 0).astype(f32).astype(bf16)
        low = (index & 255).astype(f32).astype(bf16)
        hot = jnp.where(k == low, jnp.ones((), bf16), jnp.zeros((), bf16))
        found = contract(split_ref[...], jnp.concatenate([hot, hot], axis=0), 1, 0)
        m = lax.broadcasted_iota(jnp.int32, (64, LANES), 0)
        here = m == (index >> 8)
        for part in range(4):
            rows = found[part * 64 : part * 64 + 64]
            out_ref[cluster, part : part + 1, lane : lane + LANES] = jnp.sum(
                jnp.where(here, rows, 0.0), axis=0, keepdims=True
            )

    def turn(number, carry):
        for inner in range(PICK_TURN):
            for lane in range(0, PTS, LANES):
                some_points(number * PICK_TURN + inner, lane)
        return carry

    lax.fori_loop(0, CL_DEV // PICK_TURN, turn, 0)


def pick(order, coords, weights):
    return pl.pallas_call(
        pick_kernel,
        out_shape=jax.ShapeDtypeStruct((CL_DEV, 4, PTS), f32),
        in_specs=[pl.BlockSpec(memory_space=pltpu.VMEM)] * 3,
        out_specs=pl.BlockSpec(memory_space=pltpu.VMEM),
        scratch_shapes=[pltpu.VMEM((256, 256), f32), pltpu.VMEM((256, 512), bf16)],
        compiler_params=pltpu.CompilerParams(vmem_limit_bytes=32 << 20),
        cost_estimate=pl.CostEstimate(
            flops=5_000_000_000, bytes_accessed=600_000, transcendentals=0
        ),
        name="pick",
    )(order, coords, weights)


def plan_kernel(row_ref, col_ref, slots_ref, rank_ref, wanted_ref, places_ref):
    count = rank_ref.shape[1]
    square = (count, count)
    row_owner, col_owner = row_ref[...].astype(f32), col_ref[...].astype(f32)
    row_slot, col_slot = slots_ref[0:1, :].astype(f32), slots_ref[1:2, :].astype(f32)
    rank = rank_ref[...].astype(f32)
    down = lax.broadcasted_iota(jnp.int32, square, 0)
    along = lax.broadcasted_iota(jnp.int32, square, 1)
    eye = down == along
    number = along.astype(f32)
    number_down = down.astype(f32)

    def column(row):
        return jnp.sum(jnp.where(eye, row, 0.0), axis=1, keepdims=True)

    def product(a, b):
        return jnp.where(contract(a, b, 1, 0) > 0.5, 1.0, 0.0).astype(bf16)

    same_row = jnp.where((column(row_owner) == row_owner) & ~eye, 1.0, 0.0)
    same_col = jnp.where((column(col_owner) == col_owner) & ~eye, 1.0, 0.0)
    either = (same_row + same_col).astype(bf16)
    same_row, same_col = same_row.astype(bf16), same_col.astype(bf16)
    steps = contract(same_row, same_col, 1, 0) + contract(same_col, same_row, 1, 0)
    alike = jnp.where(eye | (steps > 0.5), 1.0, 0.0).astype(bf16)
    for _ in range(4):
        alike = product(alike, alike)
    other = product(alike, either)
    far = float(2 * count)
    least = jnp.min(jnp.where(alike.astype(f32) > 0.5, number, far), axis=1, keepdims=True)
    least_other = jnp.min(jnp.where(other.astype(f32) > 0.5, number, far), axis=1, keepdims=True)
    first = jnp.where(least < least_other, 1.0, 0.0)
    size = jnp.sum(first, axis=0, keepdims=True)
    flip = size < count / 2
    first = jnp.where(flip, 1.0 - first, first)
    size = jnp.where(flip, count - size, size)
    first_row = jnp.sum(jnp.where(eye, first, 0.0), axis=0, keepdims=True)
    before = jnp.sum(jnp.where(along < down, first_row, 0.0), axis=1, keepdims=True)
    before_other = jnp.sum(jnp.where(along < down, 1.0 - first_row, 0.0), axis=1, keepdims=True)
    position = jnp.where(first > 0.5, before, size + before_other)
    hit = position == number

    def ordered(values):
        return jnp.sum(jnp.where(hit, values, 0.0), axis=0, keepdims=True)

    places = [
        ordered(number_down),
        ordered(column(row_owner * 2.0)),
        ordered(column(col_owner * 2.0 + 1.0)),
        ordered(column(rank)),
        ordered(1.0 - first),
    ]
    for line, value in enumerate(places):
        places_ref[line : line + 1, :] = value.astype(jnp.int32)
    places_ref[5:8, :] = jnp.zeros((3, count), jnp.int32)
    lane = lax.broadcasted_iota(jnp.int32, wanted_ref.shape, 1)
    wanted = jnp.zeros(wanted_ref.shape, f32)
    for phase in range(2):
        turn = first_row > 0.5 if phase == 0 else first_row < 0.5
        for side, (owner, slot) in enumerate(((row_owner, row_slot), (col_owner, col_slot))):
            value = jnp.sum(
                jnp.where((owner == number_down) & turn, slot, 0.0), axis=1, keepdims=True
            )
            wanted = jnp.where(lane == phase * 2 + side, value, wanted)
    wanted_ref[...] = wanted.astype(jnp.int32)


def plan(row_owner, col_owner, slots, rank, members):
    count = rank.shape[1]
    return pl.pallas_call(
        plan_kernel,
        out_shape=[
            jax.ShapeDtypeStruct((members, 128), jnp.int32),
            jax.ShapeDtypeStruct((8, count), jnp.int32),
        ],
        in_specs=[pl.BlockSpec(memory_space=pltpu.VMEM)] * 4,
        out_specs=[pl.BlockSpec(memory_space=pltpu.VMEM)] * 2,
        name="plan",
    )(row_owner, col_owner, slots, rank)


def reply_kernel(phase, asked_ref, points_ref, found_ref, asked_smem, asked_sem, sem):
    fetch = pltpu.make_async_copy(asked_ref, asked_smem, asked_sem)
    fetch.start()
    fetch.wait()
    for member in range(found_ref.shape[0]):
        for side in range(2):
            pltpu.make_async_copy(
                points_ref.at[asked_smem[member, phase * 2 + side]],
                found_ref.at[member, side],
                sem,
            ).start()
    pltpu.make_async_copy(found_ref, found_ref, sem).wait()


def reply(phase, asked, points):
    return pl.pallas_call(
        functools.partial(reply_kernel, phase),
        in_specs=[pl.BlockSpec(memory_space=pl.ANY), pl.BlockSpec(memory_space=pltpu.VMEM)],
        out_specs=pl.BlockSpec(memory_space=pltpu.HBM),
        out_shape=jax.ShapeDtypeStruct((asked.shape[0], 2, 4, PTS), f32),
        scratch_shapes=[
            pltpu.SMEM(asked.shape, jnp.int32),
            pltpu.SemaphoreType.DMA,
            pltpu.SemaphoreType.DMA,
        ],
        compiler_params=pltpu.CompilerParams(vmem_limit_bytes=4 << 20),
        cost_estimate=pl.CostEstimate(flops=0, bytes_accessed=4_000_000, transcendentals=0),
        name="reply",
    )(asked, points)


def split3(value):
    first = value.astype(bf16).astype(f32)
    rest = value - first
    second = rest.astype(bf16).astype(f32)
    return first, second, rest - second


def distance_operands(rows, cols):
    line = lax.broadcasted_iota(jnp.int32, (4, PTS), 0)
    row_square = rows[0:1] * rows[0:1] + rows[1:2] * rows[1:2] + rows[2:3] * rows[2:3]
    left = jnp.where(line < 3, rows, row_square)
    inverse = 1.0 / (cols[3:4] * cols[3:4])
    col_square = cols[0:1] * cols[0:1] + cols[1:2] * cols[1:2] + cols[2:3] * cols[2:3]
    right = jnp.where(line < 3, cols * (-2.0 * inverse), inverse)
    l1, l2, l3 = split3(left)
    r1, r2, r3 = split3(right)
    c1, c2, c3 = split3((col_square + softening) * inverse)
    ones = jnp.ones((4, PTS), f32)
    zero = jnp.zeros((4, PTS), f32)
    last = jnp.where(line == 0, c1, jnp.where(line == 1, c2, jnp.where(line == 2, c3, 0.0)))
    left = jnp.concatenate([l1, l1, l2, l1, l2, l3, ones, zero], axis=0).astype(bf16)
    right = jnp.concatenate([r1, r2, r1, r3, r2, r1, last, zero], axis=0).astype(bf16)
    return left, right


def pair_kernel(first, steps, phases, places, *refs):
    replies = refs[:phases]
    sketches = refs[phases : phases + 2]
    range_ref, co_ref = refs[-12:-10]
    turned, ranged = refs[-10:-8], refs[-8:-6]
    left_ref, right_ref, range_out, co_out = refs[-6:-2]
    range_sem, co_sem = refs[-2:]
    p = pl.program_id(0)
    slot = lax.rem(p, 2)
    scale = 1.0 / math.sqrt(PTS)

    def prepare(pair, side):
        row_at, col_at = places[1, pair], places[2, pair]
        rows, cols = replies[0][row_at], replies[0][col_at]
        if phases > 1:
            early = places[4, pair] == 0
            rows = jnp.where(early, rows, replies[1][row_at])
            cols = jnp.where(early, cols, replies[1][col_at])
        left, right = distance_operands(rows, cols)
        left_ref[side] = left
        right_ref[side] = right.T

    def send_range(step, side):
        at = lax.rem(step, 2)
        return pltpu.make_async_copy(
            range_out.at[at, side],
            range_ref.at[places[0, first + 2 * step + side]],
            range_sem.at[at, side],
        )

    def send_co(step, side):
        at = lax.rem(step, 2)
        return pltpu.make_async_copy(
            co_out.at[at, side],
            co_ref.at[places[0, first + 2 * step - 1 + side]],
            co_sem.at[at, side],
        )

    @pl.when(p == 0)
    def _():
        for side in range(2):
            prepare(first + side, side)

    @pl.when(p >= 2)
    def _():
        for side in range(2):
            send_range(p - 2, side).wait()
        send_co(p - 2, 1).wait()

    @pl.when(p >= 3)
    def _():
        send_co(p - 2, 0).wait()

    following = jnp.minimum(p + 1, steps - 1)
    for side in range(2):
        other = 1 - side
        left, right = left_ref[side], right_ref[side]
        limit = places[3, first + 2 * p + side] * BLK
        test = sketches[side][0]
        active = lax.broadcasted_iota(jnp.int32, (1, RK), 1) < limit
        masked = jnp.where(active, test, jnp.zeros_like(test)).T
        for start in range(0, PTS, CHUNK):
            part = slice(start, start + CHUNK)
            block = lax.rsqrt(contract(right, left[:, part], 1, 0)).astype(bf16)
            product = contract(ranged[other][...], turned[other][:, part], 1, 0)
            co_out[slot, side, :, part] = (product * scale).astype(bf16)
            if start == 0:
                prepare(first + 2 * following + side, side)
            some = contract(masked, block, 1, 0).astype(bf16)
            range_out[slot, side, part, :] = some.T
            ranged[side][:, part] = some
            turned[side][part, :] = block.T

    for side in range(2):
        send_range(p, side).start()
    send_co(p, 1).start()

    @pl.when(p >= 1)
    def _():
        send_co(p, 0).start()

    @pl.when(p == steps - 1)
    def _():
        send_co(p - 1, 0).wait()
        product = contract(ranged[1][...], turned[1][...], 1, 0)
        co_out[1 - slot, 0] = (product * scale).astype(bf16)
        send_co(p + 1, 0).start()
        for side in range(2):
            send_range(p - 1, side).wait()
            send_range(p, side).wait()
            send_co(p, side).wait()
        send_co(p - 1, 1).wait()
        send_co(p + 1, 0).wait()


def pair_products(first, number, places, replies, sketch, old):
    count = sketch.shape[0]
    steps = number // 2
    assert number == 2 * steps and steps >= 3

    def own(side):
        return lambda p, places: (places[0, first + 2 * p + side], 0, 0)

    operands = [places] + list(replies) + [sketch, sketch] + list(old)
    return pl.pallas_call(
        functools.partial(pair_kernel, first, steps, len(replies)),
        grid_spec=pltpu.PrefetchScalarGridSpec(
            num_scalar_prefetch=1,
            grid=(steps,),
            in_specs=[pl.BlockSpec(memory_space=pltpu.VMEM) for _ in replies]
            + [pl.BlockSpec((1, PTS, RK), own(side)) for side in range(2)]
            + [pl.BlockSpec(memory_space=pl.ANY) for _ in old],
            out_specs=[pl.BlockSpec(memory_space=pl.ANY)] * 2,
            scratch_shapes=[pltpu.VMEM((PTS, PTS), bf16)] * 2
            + [pltpu.VMEM((RK, PTS), bf16)] * 2
            + [
                pltpu.VMEM((2, 32, PTS), bf16),
                pltpu.VMEM((2, PTS, 32), bf16),
                pltpu.VMEM((2, 2, PTS, RK), bf16),
                pltpu.VMEM((2, 2, RK, PTS), bf16),
                pltpu.SemaphoreType.DMA((2, 2)),
                pltpu.SemaphoreType.DMA((2, 2)),
            ],
        ),
        out_shape=[
            jax.ShapeDtypeStruct((count, PTS, RK), bf16),
            jax.ShapeDtypeStruct((count, RK, PTS), bf16),
        ],
        input_output_aliases={len(operands) - 2: 0, len(operands) - 1: 1} if old else {},
        compiler_params=pltpu.CompilerParams(vmem_limit_bytes=48 << 20),
        cost_estimate=pl.CostEstimate(
            flops=number * 6 * PTS * PTS * 256, bytes_accessed=number * 800_000, transcendentals=0
        ),
        name="pairs",
    )(*operands)


def shards(
    panel_coords, panel_weights, panel_order, row_owner, col_owner, pair_slots, rank_blocks, sketch
):
    members = lax.axis_size("dev")
    count = rank_blocks.shape[0]
    wanted, places = plan(
        row_owner.reshape(1, count),
        col_owner.reshape(1, count),
        pair_slots.T,
        rank_blocks.reshape(1, count),
        members,
    )
    asked = lax.all_to_all(wanted, "dev", split_axis=0, concat_axis=0, tiled=True)
    points = pick(panel_order, panel_coords, panel_weights.reshape(128, 128))
    replies = []
    for phase in range(2):
        found = reply(phase, asked, points)
        got = lax.all_to_all(found, "dev", split_axis=0, concat_axis=0, tiled=True)
        replies.append(got.reshape(members * 2, 4, PTS))
    half = count // 2
    early = pair_products(0, half, places, replies[:1], sketch, ())
    return tuple(pair_products(half, count - half, places, replies, sketch, early))


def solution(mesh):
    in_specs = (
        P(None, ("leaf", "dev")),
        P(("leaf", "dev")),
        P(("leaf", "dev"), None),
        P(("leaf", "dev"), None),
        P(("leaf", "dev"), None),
        P(("leaf", "dev"), None),
        P(("leaf", "dev")),
        P(("leaf", "dev"), None, None),
    )
    out_specs = (P(("leaf", "dev"), None, None), P(("leaf", "dev"), None, None))
    return jax.shard_map(shards, mesh=mesh, in_specs=in_specs, out_specs=out_specs, check_vma=False)
```

```python
import functools
import math

import jax
import jax.numpy as jnp
from jax import lax
from jax.experimental import pallas as pl
from jax.experimental.pallas import tpu as pltpu
from jax.sharding import PartitionSpec as P

PTS = 1024
RK = 128
BLK = 32
CL_DEV = 16
CHUNK = 256

softening = 0.01
bf16 = jnp.bfloat16
f32 = jnp.float32


def contract(a, b, dim_a, dim_b):
    return lax.dot_general(a, b, (((dim_a,), (dim_b,)), ((), ())), preferred_element_type=f32)

PICK_TURN = 8
LANES = 256


def pick_kernel(order_ref, coords_ref, weights_ref, out_ref, table_ref, split_ref):
    for part in range(3):
        for m in range(64):
            table_ref[part * 64 + m : part * 64 + m + 1, :] = coords_ref[
                part : part + 1, m * 256 : m * 256 + 256
            ]
    for half in range(2):
        table_ref[192:256, half * 128 : half * 128 + 128] = weights_ref[
            pl.ds(half, 64, stride=2), :
        ]
    table = table_ref[...]
    head = table.astype(bf16)
    split_ref[:, 0:256] = head
    split_ref[:, 256:512] = (table - head.astype(f32)).astype(bf16)

    def some_points(cluster, lane):
        index = order_ref[0:1, pl.ds(pl.multiple_of(cluster * PTS + lane, LANES), LANES)]
        k = lax.broadcasted_iota(jnp.int32, (256, LANES), 0).astype(f32).astype(bf16)
        low = (index & 255).astype(f32).astype(bf16)
        hot = jnp.where(k == low, jnp.ones((), bf16), jnp.zeros((), bf16))
        found = contract(split_ref[...], jnp.concatenate([hot, hot], axis=0), 1, 0)
        m = lax.broadcasted_iota(jnp.int32, (64, LANES), 0)
        here = m == (index >> 8)
        for part in range(4):
            rows = found[part * 64 : part * 64 + 64]
            value = jnp.sum(jnp.where(here, rows, 0.0), axis=0, keepdims=True)
            for start in range(0, LANES, 128):
                line = part * 8 + (lane + start) // 128
                out_ref[cluster, line : line + 1, :] = value[:, start : start + 128]

    def turn(number, carry):
        for inner in range(PICK_TURN):
            for lane in range(0, PTS, LANES):
                some_points(number * PICK_TURN + inner, lane)
        return carry

    lax.fori_loop(0, CL_DEV // PICK_TURN, turn, 0)


def pick(order, coords, weights):
    return pl.pallas_call(
        pick_kernel,
        out_shape=jax.ShapeDtypeStruct((CL_DEV, 32, 128), f32),
        in_specs=[pl.BlockSpec(memory_space=pltpu.VMEM)] * 3,
        out_specs=pl.BlockSpec(memory_space=pltpu.VMEM),
        scratch_shapes=[pltpu.VMEM((256, 256), f32), pltpu.VMEM((256, 512), bf16)],
        compiler_params=pltpu.CompilerParams(vmem_limit_bytes=32 << 20),
        cost_estimate=pl.CostEstimate(
            flops=5_000_000_000, bytes_accessed=600_000, transcendentals=0
        ),
        name="pick",
    )(order, coords, weights)


def plan_kernel(row_ref, col_ref, slots_ref, rank_ref, wanted_ref, places_ref):
    count = rank_ref.shape[1]
    square = (count, count)
    row_owner, col_owner = row_ref[...].astype(f32), col_ref[...].astype(f32)
    row_slot, col_slot = slots_ref[0:1, :].astype(f32), slots_ref[1:2, :].astype(f32)
    rank = rank_ref[...].astype(f32)
    down = lax.broadcasted_iota(jnp.int32, square, 0)
    along = lax.broadcasted_iota(jnp.int32, square, 1)
    eye = down == along
    number = along.astype(f32)
    number_down = down.astype(f32)

    def column(row):
        return jnp.sum(jnp.where(eye, row, 0.0), axis=1, keepdims=True)

    def product(a, b):
        return jnp.where(contract(a, b, 1, 0) > 0.5, 1.0, 0.0).astype(bf16)

    same_row = jnp.where((column(row_owner) == row_owner) & ~eye, 1.0, 0.0)
    same_col = jnp.where((column(col_owner) == col_owner) & ~eye, 1.0, 0.0)
    either = (same_row + same_col).astype(bf16)
    same_row, same_col = same_row.astype(bf16), same_col.astype(bf16)
    steps = contract(same_row, same_col, 1, 0) + contract(same_col, same_row, 1, 0)
    alike = jnp.where(eye | (steps > 0.5), 1.0, 0.0).astype(bf16)
    for _ in range(4):
        alike = product(alike, alike)
    other = product(alike, either)
    far = float(2 * count)
    least = jnp.min(jnp.where(alike.astype(f32) > 0.5, number, far), axis=1, keepdims=True)
    least_other = jnp.min(jnp.where(other.astype(f32) > 0.5, number, far), axis=1, keepdims=True)
    first = jnp.where(least < least_other, 1.0, 0.0)
    size = jnp.sum(first, axis=0, keepdims=True)
    flip = size < count / 2
    first = jnp.where(flip, 1.0 - first, first)
    size = jnp.where(flip, count - size, size)
    first_row = jnp.sum(jnp.where(eye, first, 0.0), axis=0, keepdims=True)
    before = jnp.sum(jnp.where(along < down, first_row, 0.0), axis=1, keepdims=True)
    before_other = jnp.sum(jnp.where(along < down, 1.0 - first_row, 0.0), axis=1, keepdims=True)
    position = jnp.where(first > 0.5, before, size + before_other)
    hit = position == number

    def ordered(values):
        return jnp.sum(jnp.where(hit, values, 0.0), axis=0, keepdims=True)

    places = [
        ordered(number_down),
        ordered(column(row_owner)),
        ordered(column(col_owner)),
        ordered(column(rank)),
        ordered(1.0 - first),
    ]
    for line, value in enumerate(places):
        places_ref[line : line + 1, :] = value.astype(jnp.int32)
    places_ref[5:8, :] = jnp.zeros((3, count), jnp.int32)
    lane = lax.broadcasted_iota(jnp.int32, wanted_ref.shape, 1)
    wanted = jnp.zeros(wanted_ref.shape, f32)
    for phase in range(2):
        turn = first_row > 0.5 if phase == 0 else first_row < 0.5
        for side, (owner, slot) in enumerate(((row_owner, row_slot), (col_owner, col_slot))):
            value = jnp.sum(
                jnp.where((owner == number_down) & turn, slot, 0.0), axis=1, keepdims=True
            )
            wanted = jnp.where(lane == phase * 2 + side, value, wanted)
    wanted_ref[...] = wanted.astype(jnp.int32)


def plan(row_owner, col_owner, slots, rank, members):
    count = rank.shape[1]
    return pl.pallas_call(
        plan_kernel,
        out_shape=[
            jax.ShapeDtypeStruct((members, 128), jnp.int32),
            jax.ShapeDtypeStruct((8, count), jnp.int32),
        ],
        in_specs=[pl.BlockSpec(memory_space=pltpu.VMEM)] * 4,
        out_specs=[pl.BlockSpec(memory_space=pltpu.VMEM)] * 2,
        name="plan",
    )(row_owner, col_owner, slots, rank)


def reply_kernel(phase, asked_ref, points_ref, found_ref, asked_smem, asked_sem, sem):
    fetch = pltpu.make_async_copy(asked_ref, asked_smem, asked_sem)
    fetch.start()
    fetch.wait()
    for member in range(found_ref.shape[0]):
        for side, (start, size) in enumerate(((0, 24), (24, 32))):
            pltpu.make_async_copy(
                points_ref.at[asked_smem[member, phase * 2 + side], pl.ds(0, size)],
                found_ref.at[member, pl.ds(start, size)],
                sem,
            ).start()
    pltpu.make_async_copy(found_ref, found_ref, sem).wait()


def reply(phase, asked, points):
    return pl.pallas_call(
        functools.partial(reply_kernel, phase),
        in_specs=[pl.BlockSpec(memory_space=pl.ANY), pl.BlockSpec(memory_space=pltpu.VMEM)],
        out_specs=pl.BlockSpec(memory_space=pltpu.HBM),
        out_shape=jax.ShapeDtypeStruct((asked.shape[0], 56, 128), f32),
        scratch_shapes=[
            pltpu.SMEM(asked.shape, jnp.int32),
            pltpu.SemaphoreType.DMA,
            pltpu.SemaphoreType.DMA,
        ],
        compiler_params=pltpu.CompilerParams(vmem_limit_bytes=4 << 20),
        cost_estimate=pl.CostEstimate(flops=0, bytes_accessed=4_000_000, transcendentals=0),
        name="reply",
    )(asked, points)


def split3(value):
    first = value.astype(bf16).astype(f32)
    rest = value - first
    second = rest.astype(bf16).astype(f32)
    return first, second, rest - second


def distance_operands(rows, cols):
    line = lax.broadcasted_iota(jnp.int32, (4, PTS), 0)
    row_square = rows[0:1] * rows[0:1] + rows[1:2] * rows[1:2] + rows[2:3] * rows[2:3]
    left = jnp.where(line < 3, rows, row_square)
    inverse = 1.0 / (cols[3:4] * cols[3:4])
    col_square = cols[0:1] * cols[0:1] + cols[1:2] * cols[1:2] + cols[2:3] * cols[2:3]
    right = jnp.where(line < 3, cols * (-2.0 * inverse), inverse)
    l1, l2, l3 = split3(left)
    r1, r2, r3 = split3(right)
    c1, c2, c3 = split3((col_square + softening) * inverse)
    ones = jnp.ones((4, PTS), f32)
    zero = jnp.zeros((4, PTS), f32)
    last = jnp.where(line == 0, c1, jnp.where(line == 1, c2, jnp.where(line == 2, c3, 0.0)))
    left = jnp.concatenate([l1, l1, l2, l1, l2, l3, ones, zero], axis=0).astype(bf16)
    right = jnp.concatenate([r1, r2, r1, r3, r2, r1, last, zero], axis=0).astype(bf16)
    return left, right


def pair_kernel(first, steps, phases, places, *refs):
    replies = refs[:phases]
    sketches = refs[phases : phases + 2]
    range_ref, co_ref = refs[-12:-10]
    turned, ranged = refs[-10:-8], refs[-8:-6]
    left_ref, right_ref, range_out, co_out = refs[-6:-2]
    range_sem, co_sem = refs[-2:]
    p = pl.program_id(0)
    slot = lax.rem(p, 2)
    scale = 1.0 / math.sqrt(PTS)

    def cluster(reply_ref, at, start):
        return jnp.concatenate(
            [reply_ref[at, pl.ds(start + line, 4, stride=8), :] for line in range(8)], axis=1
        )

    def prepare(pair, side):
        row_at, col_at = places[1, pair], places[2, pair]
        rows, cols = cluster(replies[0], row_at, 0), cluster(replies[0], col_at, 24)
        if phases > 1:
            early = places[4, pair] == 0
            rows = jnp.where(early, rows, cluster(replies[1], row_at, 0))
            cols = jnp.where(early, cols, cluster(replies[1], col_at, 24))
        left, right = distance_operands(rows, cols)
        left_ref[side] = left
        right_ref[side] = right.T

    def send_range(step, side):
        at = lax.rem(step, 2)
        return pltpu.make_async_copy(
            range_out.at[at, side],
            range_ref.at[places[0, first + 2 * step + side]],
            range_sem.at[at, side],
        )

    def send_co(step, side):
        at = lax.rem(step, 2)
        return pltpu.make_async_copy(
            co_out.at[at, side],
            co_ref.at[places[0, first + 2 * step - 1 + side]],
            co_sem.at[at, side],
        )

    @pl.when(p == 0)
    def _():
        for side in range(2):
            prepare(first + side, side)

    @pl.when(p >= 2)
    def _():
        for side in range(2):
            send_range(p - 2, side).wait()
        send_co(p - 2, 1).wait()

    @pl.when(p >= 3)
    def _():
        send_co(p - 2, 0).wait()

    following = jnp.minimum(p + 1, steps - 1)
    for side in range(2):
        other = 1 - side
        left, right = left_ref[side], right_ref[side]
        limit = places[3, first + 2 * p + side] * BLK
        test = sketches[side][0]
        active = lax.broadcasted_iota(jnp.int32, (1, RK), 1) < limit
        masked = jnp.where(active, test, jnp.zeros_like(test)).T
        for start in range(0, PTS, CHUNK):
            part = slice(start, start + CHUNK)
            block = lax.rsqrt(contract(right, left[:, part], 1, 0)).astype(bf16)
            product = contract(ranged[other][...], turned[other][:, part], 1, 0)
            co_out[slot, side, :, part] = (product * scale).astype(bf16)
            if start == 0:
                prepare(first + 2 * following + side, side)
            some = contract(masked, block, 1, 0).astype(bf16)
            range_out[slot, side, part, :] = some.T
            ranged[side][:, part] = some
            turned[side][part, :] = block.T

    for side in range(2):
        send_range(p, side).start()
    send_co(p, 1).start()

    @pl.when(p >= 1)
    def _():
        send_co(p, 0).start()

    @pl.when(p == steps - 1)
    def _():
        send_co(p - 1, 0).wait()
        product = contract(ranged[1][...], turned[1][...], 1, 0)
        co_out[1 - slot, 0] = (product * scale).astype(bf16)
        send_co(p + 1, 0).start()
        for side in range(2):
            send_range(p - 1, side).wait()
            send_range(p, side).wait()
            send_co(p, side).wait()
        send_co(p - 1, 1).wait()
        send_co(p + 1, 0).wait()


def pair_products(first, number, places, replies, sketch, old):
    count = sketch.shape[0]
    steps = number // 2
    assert number == 2 * steps and steps >= 3

    def own(side):
        return lambda p, places: (places[0, first + 2 * p + side], 0, 0)

    operands = [places] + list(replies) + [sketch, sketch] + list(old)
    return pl.pallas_call(
        functools.partial(pair_kernel, first, steps, len(replies)),
        grid_spec=pltpu.PrefetchScalarGridSpec(
            num_scalar_prefetch=1,
            grid=(steps,),
            in_specs=[pl.BlockSpec(memory_space=pltpu.VMEM) for _ in replies]
            + [pl.BlockSpec((1, PTS, RK), own(side)) for side in range(2)]
            + [pl.BlockSpec(memory_space=pl.ANY) for _ in old],
            out_specs=[pl.BlockSpec(memory_space=pl.ANY)] * 2,
            scratch_shapes=[pltpu.VMEM((PTS, PTS), bf16)] * 2
            + [pltpu.VMEM((RK, PTS), bf16)] * 2
            + [
                pltpu.VMEM((2, 32, PTS), bf16),
                pltpu.VMEM((2, PTS, 32), bf16),
                pltpu.VMEM((2, 2, PTS, RK), bf16),
                pltpu.VMEM((2, 2, RK, PTS), bf16),
                pltpu.SemaphoreType.DMA((2, 2)),
                pltpu.SemaphoreType.DMA((2, 2)),
            ],
        ),
        out_shape=[
            jax.ShapeDtypeStruct((count, PTS, RK), bf16),
            jax.ShapeDtypeStruct((count, RK, PTS), bf16),
        ],
        input_output_aliases={len(operands) - 2: 0, len(operands) - 1: 1} if old else {},
        compiler_params=pltpu.CompilerParams(vmem_limit_bytes=48 << 20),
        cost_estimate=pl.CostEstimate(
            flops=number * 6 * PTS * PTS * 256, bytes_accessed=number * 800_000, transcendentals=0
        ),
        name="pairs",
    )(*operands)


def shards(
    panel_coords, panel_weights, panel_order, row_owner, col_owner, pair_slots, rank_blocks, sketch
):
    members = lax.axis_size("dev")
    count = rank_blocks.shape[0]
    wanted, places = plan(
        row_owner.reshape(1, count),
        col_owner.reshape(1, count),
        pair_slots.T,
        rank_blocks.reshape(1, count),
        members,
    )
    asked = lax.all_to_all(wanted, "dev", split_axis=0, concat_axis=0, tiled=True)
    points = pick(panel_order, panel_coords, panel_weights.reshape(128, 128))
    replies = []
    for phase in range(2):
        found = reply(phase, asked, points)
        got = lax.all_to_all(found, "dev", split_axis=0, concat_axis=0, tiled=True)
        replies.append(got)
    half = count // 2
    early = pair_products(0, half, places, replies[:1], sketch, ())
    return tuple(pair_products(half, count - half, places, replies, sketch, early))


def solution(mesh):
    in_specs = (
        P(None, ("leaf", "dev")),
        P(("leaf", "dev")),
        P(("leaf", "dev"), None),
        P(("leaf", "dev"), None),
        P(("leaf", "dev"), None),
        P(("leaf", "dev"), None),
        P(("leaf", "dev")),
        P(("leaf", "dev"), None, None),
    )
    out_specs = (P(("leaf", "dev"), None, None), P(("leaf", "dev"), None, None))
    return jax.shard_map(shards, mesh=mesh, in_specs=in_specs, out_specs=out_specs, check_vma=False)
```

```python
import functools
import math

import jax
import jax.numpy as jnp
from jax import lax
from jax.experimental import pallas as pl
from jax.experimental.pallas import tpu as pltpu
from jax.sharding import PartitionSpec as P

PTS = 1024
RK = 128
BLK = 32
CL_DEV = 16
CHUNK = 256

softening = 0.01
bf16 = jnp.bfloat16
f32 = jnp.float32


def contract(a, b, dim_a, dim_b):
    return lax.dot_general(a, b, (((dim_a,), (dim_b,)), ((), ())), preferred_element_type=f32)

PICK_TURN = 16
LANES = 256


def pick_kernel(order_ref, coords_ref, weights_ref, out_ref, table_ref, split_ref):
    for part in range(3):
        for m in range(64):
            table_ref[part * 64 + m : part * 64 + m + 1, :] = coords_ref[
                part : part + 1, m * 256 : m * 256 + 256
            ]
    for half in range(2):
        table_ref[192:256, half * 128 : half * 128 + 128] = weights_ref[
            pl.ds(half, 64, stride=2), :
        ]
    table = table_ref[...]
    head = table.astype(bf16)
    split_ref[:, 0:256] = head
    split_ref[:, 256:512] = (table - head.astype(f32)).astype(bf16)

    def some_points(cluster, lane):
        index = order_ref[0:1, pl.ds(pl.multiple_of(cluster * PTS + lane, LANES), LANES)]
        k = lax.broadcasted_iota(jnp.int32, (256, LANES), 0).astype(f32).astype(bf16)
        low = (index & 255).astype(f32).astype(bf16)
        hot = jnp.where(k == low, jnp.ones((), bf16), jnp.zeros((), bf16))
        found = contract(split_ref[...], jnp.concatenate([hot, hot], axis=0), 1, 0)
        m = lax.broadcasted_iota(jnp.int32, (64, LANES), 0)
        here = m == (index >> 8)
        for part in range(4):
            rows = found[part * 64 : part * 64 + 64]
            value = jnp.sum(jnp.where(here, rows, 0.0), axis=0, keepdims=True)
            for start in range(0, LANES, 128):
                line = part * 8 + (lane + start) // 128
                out_ref[cluster, line : line + 1, :] = value[:, start : start + 128]

    def turn(number, carry):
        for inner in range(PICK_TURN):
            for lane in range(0, PTS, LANES):
                some_points(number * PICK_TURN + inner, lane)
        return carry

    lax.fori_loop(0, CL_DEV // PICK_TURN, turn, 0)


def pick(order, coords, weights):
    return pl.pallas_call(
        pick_kernel,
        out_shape=jax.ShapeDtypeStruct((CL_DEV, 32, 128), f32),
        in_specs=[pl.BlockSpec(memory_space=pltpu.VMEM)] * 3,
        out_specs=pl.BlockSpec(memory_space=pltpu.VMEM),
        scratch_shapes=[pltpu.VMEM((256, 256), f32), pltpu.VMEM((256, 512), bf16)],
        compiler_params=pltpu.CompilerParams(vmem_limit_bytes=32 << 20),
        cost_estimate=pl.CostEstimate(
            flops=5_000_000_000, bytes_accessed=600_000, transcendentals=0
        ),
        name="pick",
    )(order, coords, weights)


def plan_kernel(row_ref, col_ref, slots_ref, rank_ref, wanted_ref, places_ref):
    count = rank_ref.shape[1]
    square = (count, count)
    row_owner, col_owner = row_ref[...].astype(f32), col_ref[...].astype(f32)
    row_slot, col_slot = slots_ref[0:1, :].astype(f32), slots_ref[1:2, :].astype(f32)
    rank = rank_ref[...].astype(f32)
    down = lax.broadcasted_iota(jnp.int32, square, 0)
    along = lax.broadcasted_iota(jnp.int32, square, 1)
    eye = down == along
    number = along.astype(f32)
    number_down = down.astype(f32)

    def column(row):
        return jnp.sum(jnp.where(eye, row, 0.0), axis=1, keepdims=True)

    def product(a, b):
        return jnp.where(contract(a, b, 1, 0) > 0.5, 1.0, 0.0).astype(bf16)

    same_row = jnp.where((column(row_owner) == row_owner) & ~eye, 1.0, 0.0)
    same_col = jnp.where((column(col_owner) == col_owner) & ~eye, 1.0, 0.0)
    either = (same_row + same_col).astype(bf16)
    same_row, same_col = same_row.astype(bf16), same_col.astype(bf16)
    steps = contract(same_row, same_col, 1, 0) + contract(same_col, same_row, 1, 0)
    alike = jnp.where(eye | (steps > 0.5), 1.0, 0.0).astype(bf16)
    for _ in range(4):
        alike = product(alike, alike)
    other = product(alike, either)
    far = float(2 * count)
    least = jnp.min(jnp.where(alike.astype(f32) > 0.5, number, far), axis=1, keepdims=True)
    least_other = jnp.min(jnp.where(other.astype(f32) > 0.5, number, far), axis=1, keepdims=True)
    first = jnp.where(least < least_other, 1.0, 0.0)
    size = jnp.sum(first, axis=0, keepdims=True)
    flip = size < count / 2
    first = jnp.where(flip, 1.0 - first, first)
    size = jnp.where(flip, count - size, size)
    first_row = jnp.sum(jnp.where(eye, first, 0.0), axis=0, keepdims=True)
    before = jnp.sum(jnp.where(along < down, first_row, 0.0), axis=1, keepdims=True)
    before_other = jnp.sum(jnp.where(along < down, 1.0 - first_row, 0.0), axis=1, keepdims=True)
    position = jnp.where(first > 0.5, before, size + before_other)
    hit = position == number

    def ordered(values):
        return jnp.sum(jnp.where(hit, values, 0.0), axis=0, keepdims=True)

    places = [
        ordered(number_down),
        ordered(column(row_owner)),
        ordered(column(col_owner)),
        ordered(column(rank)),
        ordered(1.0 - first),
    ]
    for line, value in enumerate(places):
        places_ref[line : line + 1, :] = value.astype(jnp.int32)
    places_ref[5:8, :] = jnp.zeros((3, count), jnp.int32)
    lane = lax.broadcasted_iota(jnp.int32, wanted_ref.shape, 1)
    wanted = jnp.zeros(wanted_ref.shape, f32)
    for phase in range(2):
        turn = first_row > 0.5 if phase == 0 else first_row < 0.5
        for side, (owner, slot) in enumerate(((row_owner, row_slot), (col_owner, col_slot))):
            value = jnp.sum(
                jnp.where((owner == number_down) & turn, slot, 0.0), axis=1, keepdims=True
            )
            wanted = jnp.where(lane == phase * 2 + side, value, wanted)
    wanted_ref[...] = wanted.astype(jnp.int32)


def plan(row_owner, col_owner, slots, rank, members):
    count = rank.shape[1]
    return pl.pallas_call(
        plan_kernel,
        out_shape=[
            jax.ShapeDtypeStruct((members, 128), jnp.int32),
            jax.ShapeDtypeStruct((8, count), jnp.int32),
        ],
        in_specs=[pl.BlockSpec(memory_space=pltpu.VMEM)] * 4,
        out_specs=[pl.BlockSpec(memory_space=pltpu.VMEM)] * 2,
        name="plan",
    )(row_owner, col_owner, slots, rank)


def reply_kernel(phase, asked_ref, points_ref, found_ref, asked_smem, asked_sem, sem):
    fetch = pltpu.make_async_copy(asked_ref, asked_smem, asked_sem)
    fetch.start()
    fetch.wait()
    for member in range(found_ref.shape[0]):
        for side, (start, size) in enumerate(((0, 24), (24, 32))):
            pltpu.make_async_copy(
                points_ref.at[asked_smem[member, phase * 2 + side], pl.ds(0, size)],
                found_ref.at[member, pl.ds(start, size)],
                sem,
            ).start()
    pltpu.make_async_copy(found_ref, found_ref, sem).wait()


def reply(phase, asked, points):
    return pl.pallas_call(
        functools.partial(reply_kernel, phase),
        in_specs=[pl.BlockSpec(memory_space=pl.ANY), pl.BlockSpec(memory_space=pltpu.VMEM)],
        out_specs=pl.BlockSpec(memory_space=pltpu.HBM),
        out_shape=jax.ShapeDtypeStruct((asked.shape[0], 56, 128), f32),
        scratch_shapes=[
            pltpu.SMEM(asked.shape, jnp.int32),
            pltpu.SemaphoreType.DMA,
            pltpu.SemaphoreType.DMA,
        ],
        compiler_params=pltpu.CompilerParams(vmem_limit_bytes=4 << 20),
        cost_estimate=pl.CostEstimate(flops=0, bytes_accessed=4_000_000, transcendentals=0),
        name="reply",
    )(asked, points)


def split3(value):
    first = value.astype(bf16).astype(f32)
    rest = value - first
    second = rest.astype(bf16).astype(f32)
    return first, second, rest - second


def distance_operands(rows, cols):
    line = lax.broadcasted_iota(jnp.int32, (4, PTS), 0)
    row_square = rows[0:1] * rows[0:1] + rows[1:2] * rows[1:2] + rows[2:3] * rows[2:3]
    left = jnp.where(line < 3, rows, row_square)
    inverse = 1.0 / (cols[3:4] * cols[3:4])
    col_square = cols[0:1] * cols[0:1] + cols[1:2] * cols[1:2] + cols[2:3] * cols[2:3]
    right = jnp.where(line < 3, cols * (-2.0 * inverse), inverse)
    l1, l2, l3 = split3(left)
    r1, r2, r3 = split3(right)
    c1, c2, c3 = split3((col_square + softening) * inverse)
    ones = jnp.ones((4, PTS), f32)
    zero = jnp.zeros((4, PTS), f32)
    last = jnp.where(line == 0, c1, jnp.where(line == 1, c2, jnp.where(line == 2, c3, 0.0)))
    left = jnp.concatenate([l1, l1, l2, l1, l2, l3, ones, zero], axis=0).astype(bf16)
    right = jnp.concatenate([r1, r2, r1, r3, r2, r1, last, zero], axis=0).astype(bf16)
    return left, right


def pair_kernel(first, steps, phases, places, *refs):
    replies = refs[:phases]
    sketches = refs[phases : phases + 2]
    range_ref, co_ref = refs[-12:-10]
    turned, ranged = refs[-10:-8], refs[-8:-6]
    left_ref, right_ref, range_out, co_out = refs[-6:-2]
    range_sem, co_sem = refs[-2:]
    p = pl.program_id(0)
    slot = lax.rem(p, 2)
    scale = 1.0 / math.sqrt(PTS)

    def cluster(reply_ref, at, start):
        return jnp.concatenate(
            [reply_ref[at, pl.ds(start + line, 4, stride=8), :] for line in range(8)], axis=1
        )

    def prepare(pair, side):
        row_at, col_at = places[1, pair], places[2, pair]
        rows, cols = cluster(replies[0], row_at, 0), cluster(replies[0], col_at, 24)
        if phases > 1:
            early = places[4, pair] == 0
            rows = jnp.where(early, rows, cluster(replies[1], row_at, 0))
            cols = jnp.where(early, cols, cluster(replies[1], col_at, 24))
        left, right = distance_operands(rows, cols)
        left_ref[side] = left
        right_ref[side] = right.T

    def send_range(step, side):
        at = lax.rem(step, 2)
        return pltpu.make_async_copy(
            range_out.at[at, side],
            range_ref.at[places[0, first + 2 * step + side]],
            range_sem.at[at, side],
        )

    def send_co(step, side):
        at = lax.rem(step, 2)
        return pltpu.make_async_copy(
            co_out.at[at, side],
            co_ref.at[places[0, first + 2 * step - 1 + side]],
            co_sem.at[at, side],
        )

    @pl.when(p == 0)
    def _():
        for side in range(2):
            prepare(first + side, side)

    @pl.when(p >= 2)
    def _():
        for side in range(2):
            send_range(p - 2, side).wait()
        send_co(p - 2, 1).wait()

    @pl.when(p >= 3)
    def _():
        send_co(p - 2, 0).wait()

    following = jnp.minimum(p + 1, steps - 1)
    for side in range(2):
        other = 1 - side
        left, right = left_ref[side], right_ref[side]
        limit = places[3, first + 2 * p + side] * BLK
        test = sketches[side][0]
        active = lax.broadcasted_iota(jnp.int32, (1, RK), 1) < limit
        masked = jnp.where(active, test, jnp.zeros_like(test)).T
        for start in range(0, PTS, CHUNK):
            part = slice(start, start + CHUNK)
            block = lax.rsqrt(contract(right, left[:, part], 1, 0)).astype(bf16)
            product = contract(ranged[other][...], turned[other][:, part], 1, 0)
            co_out[slot, side, :, part] = (product * scale).astype(bf16)
            if start == 0:
                prepare(first + 2 * following + side, side)
            some = contract(masked, block, 1, 0).astype(bf16)
            range_out[slot, side, part, :] = some.T
            ranged[side][:, part] = some
            turned[side][part, :] = block.T

    for side in range(2):
        send_range(p, side).start()
    send_co(p, 1).start()

    @pl.when(p >= 1)
    def _():
        send_co(p, 0).start()

    @pl.when(p == steps - 1)
    def _():
        send_co(p - 1, 0).wait()
        product = contract(ranged[1][...], turned[1][...], 1, 0)
        co_out[1 - slot, 0] = (product * scale).astype(bf16)
        send_co(p + 1, 0).start()
        for side in range(2):
            send_range(p - 1, side).wait()
            send_range(p, side).wait()
            send_co(p, side).wait()
        send_co(p - 1, 1).wait()
        send_co(p + 1, 0).wait()


def pair_products(first, number, places, replies, sketch, old):
    count = sketch.shape[0]
    steps = number // 2
    assert number == 2 * steps and steps >= 3

    def own(side):
        return lambda p, places: (places[0, first + 2 * p + side], 0, 0)

    operands = [places] + list(replies) + [sketch, sketch] + list(old)
    return pl.pallas_call(
        functools.partial(pair_kernel, first, steps, len(replies)),
        grid_spec=pltpu.PrefetchScalarGridSpec(
            num_scalar_prefetch=1,
            grid=(steps,),
            in_specs=[pl.BlockSpec(memory_space=pltpu.VMEM) for _ in replies]
            + [pl.BlockSpec((1, PTS, RK), own(side)) for side in range(2)]
            + [pl.BlockSpec(memory_space=pl.ANY) for _ in old],
            out_specs=[pl.BlockSpec(memory_space=pl.ANY)] * 2,
            scratch_shapes=[pltpu.VMEM((PTS, PTS), bf16)] * 2
            + [pltpu.VMEM((RK, PTS), bf16)] * 2
            + [
                pltpu.VMEM((2, 32, PTS), bf16),
                pltpu.VMEM((2, PTS, 32), bf16),
                pltpu.VMEM((2, 2, PTS, RK), bf16),
                pltpu.VMEM((2, 2, RK, PTS), bf16),
                pltpu.SemaphoreType.DMA((2, 2)),
                pltpu.SemaphoreType.DMA((2, 2)),
            ],
        ),
        out_shape=[
            jax.ShapeDtypeStruct((count, PTS, RK), bf16),
            jax.ShapeDtypeStruct((count, RK, PTS), bf16),
        ],
        input_output_aliases={len(operands) - 2: 0, len(operands) - 1: 1} if old else {},
        compiler_params=pltpu.CompilerParams(vmem_limit_bytes=48 << 20),
        cost_estimate=pl.CostEstimate(
            flops=number * 6 * PTS * PTS * 256, bytes_accessed=number * 800_000, transcendentals=0
        ),
        name="pairs",
    )(*operands)


def shards(
    panel_coords, panel_weights, panel_order, row_owner, col_owner, pair_slots, rank_blocks, sketch
):
    members = lax.axis_size("dev")
    count = rank_blocks.shape[0]
    wanted, places = plan(
        row_owner.reshape(1, count),
        col_owner.reshape(1, count),
        pair_slots.T,
        rank_blocks.reshape(1, count),
        members,
    )
    asked = lax.all_to_all(wanted, "dev", split_axis=0, concat_axis=0, tiled=True)
    points = pick(panel_order, panel_coords, panel_weights.reshape(128, 128))
    replies = []
    for phase in range(2):
        found = reply(phase, asked, points)
        got = lax.all_to_all(found, "dev", split_axis=0, concat_axis=0, tiled=True)
        replies.append(got)
    half = count // 2
    early = pair_products(0, half, places, replies[:1], sketch, ())
    return tuple(pair_products(half, count - half, places, replies, sketch, early))


def solution(mesh):
    in_specs = (
        P(None, ("leaf", "dev")),
        P(("leaf", "dev")),
        P(("leaf", "dev"), None),
        P(("leaf", "dev"), None),
        P(("leaf", "dev"), None),
        P(("leaf", "dev"), None),
        P(("leaf", "dev")),
        P(("leaf", "dev"), None, None),
    )
    out_specs = (P(("leaf", "dev"), None, None), P(("leaf", "dev"), None, None))
    return jax.shard_map(shards, mesh=mesh, in_specs=in_specs, out_specs=out_specs, check_vma=False)
```
